128 devices in a mesh: gx: 16 (over y_hi, x, core), gy: 8 (over z, y_lo).
Axes of the slice: x: 4, y: 4 (y_hi: 2, y_lo: 2; y = y_hi * 2 + y_lo), z: 4, core: 2. Of those that a mesh axis runs over, the one named last changes fastest.
Arguments:
- tendencies: bfloat16 [8192, 2, 24, 16, 128], P(('gx', 'gy')), may hold values from -6 to 6
- thickness: float32 [24], replicated, may hold values from 0.1 to 0.4
- ocean_blocks: int32 [8192], replicated, may hold values from 0 to 10239, as said below
- land_mask: int32 [2560, 8192], P('gy', 'gx'), may hold values from 0 to 1, as said below
- implicit_term: float32 [2560, 8192], P('gy', 'gx'), may hold values from 0.05 to 0.5
- first_guess: float32 [2560, 8192], P('gy', 'gx'), may hold values from -6 to 6
Outputs:
- solution: float32 [2560, 8192], P('gy', 'gx')
- residual: float32 [2560, 8192], P('gy', 'gx')
- gradient_blocks: float32 [8192, 2, 16, 128], P(('gx', 'gy'))
The draws below stay inside these ranges and needn't reach their ends.
Inputs may be any that keep to these rules, and one draw needn't show every extreme that they name: `ocean_blocks`: distinct global indices p * 64 + q of ocean blocks (block row p, block column q). Every device's tile holds exactly 64 listed blocks, and the 64 entries that one device holds lie in the tiles of exactly 64 devices, 1 in each. `land_mask`: every cell of a block that ocean_blocks does not list is 0.
All inputs are finite; a program needn't handle non-finite values.
Results may differ from the reference program's by a relative error of at most 0.0003.
Values sent between devices are 32-bit elements; how exact they have to be, the bound alone decides.
No kernel may reach another device: no remote copies, remote signals or barrier semaphores. Data moves between devices by JAX's collectives and lax.ppermute only.
A program may use at most 128 MiB of HBM per device.

```python
import math
import jax
import jax.numpy as jnp

BX = 128
BY = 16
BCOL = 4
BROW = 20
LEV = 24
ITERS = 4
OCEAN_BLOCKS = 8192
NX = 8192
NY = 2560
N_GX = 16
N_GY = 8


def ocean_layout(key):
    devices = N_GX * N_GY
    tile_blocks = BCOL * BROW
    ocean_count = tile_blocks - tile_blocks // 5
    capacity = max(1, 2 * ocean_count // devices)
    fanout = ocean_count // capacity
    key_pick, key_label, key_shift, key_shuffle = jax.random.split(key, 4)
    scores = jax.random.randint(key_pick, (devices, tile_blocks), 0, 1 << 20) * tile_blocks + jnp.arange(tile_blocks, dtype=jnp.int32)[None, :]
    scores = scores.at[0, 0].set(-1).at[devices - 1, tile_blocks - 1].set(-1)
    chosen = jnp.argsort(scores, axis=1)[:, :ocean_count].astype(jnp.int32)
    relabel = jax.random.permutation(key_label, devices).astype(jnp.int32)
    placement_of = jnp.argsort(relabel).astype(jnp.int32)
    shifts = jax.random.permutation(key_shift, devices)[:fanout].astype(jnp.int32)
    sources = jnp.arange(devices, dtype=jnp.int32)
    targets = relabel[(placement_of[sources][:, None] + shifts[None, :]) % devices]
    slot_index = jnp.arange(fanout, dtype=jnp.int32)[:, None] * capacity + jnp.arange(capacity, dtype=jnp.int32)[None, :]
    local_ids = chosen[targets[:, :, None], slot_index[None, :, :]]
    target_all = jnp.broadcast_to(targets[:, :, None], local_ids.shape)
    tile_row = target_all % N_GY
    tile_col = target_all // N_GY
    block_row = tile_row * BROW + local_ids // BCOL
    block_col = tile_col * BCOL + local_ids % BCOL
    global_ids = (block_row * (BCOL * N_GX) + block_col).reshape(devices, ocean_count)
    shuffle_scores = jax.random.randint(key_shuffle, (devices, ocean_count), 0, 1 << 20) * ocean_count + jnp.arange(ocean_count, dtype=jnp.int32)[None, :]
    shuffle = jnp.argsort(shuffle_scores, axis=1)
    return jnp.take_along_axis(global_ids, shuffle, axis=1).reshape(-1).astype(jnp.int32)


def draw_ocean_blocks(key, part):
    return ocean_layout(key)


def draw_land_mask(key, part):
    listed = ocean_layout(key)
    key = jax.random.fold_in(key, 7)
    total_blocks = BROW * N_GY * BCOL * N_GX
    flags = jnp.zeros((total_blocks,), jnp.int32).at[listed].set(1).reshape(BROW * N_GY, BCOL * N_GX)
    cells = jnp.repeat(jnp.repeat(flags, BY, axis=0), BX, axis=1)
    coast = (jax.random.randint(key, cells.shape, 0, 10) > 0).astype(jnp.int32)
    return cells * coast


def shard_levels(rng, shape, cuts, smallest, top_value):
    loudness, own = 1.0, jax.random.fold_in(rng, 6)
    for dim, parts in cuts:
        draws = jnp.exp(jax.random.uniform(jax.random.fold_in(own, dim), (parts,), jnp.float32, smallest / len(cuts), top_value / len(cuts)))
        loudness = loudness * jnp.repeat(draws, shape[dim] // parts).reshape([-1 if axis == dim else 1 for axis in range(len(shape))])
    return loudness


def centred(key, dims, width, reach, cuts=(), kind=jnp.bfloat16):
    entries = jax.random.normal(key, dims, jnp.float32) * width
    if len(cuts) > 0:
        entries = shard_levels(key, dims, cuts, -0.22, 0.18) * entries
    return jnp.clip(entries, min=-reach, max=reach).astype(kind)


def setup_inputs(seed: int = 0) -> dict:
    keys = jax.random.split(jax.random.key(seed), 7)
    tendencies = centred(keys[0], (OCEAN_BLOCKS, 2, LEV, BY, BX), 1.0, 6.0, ((0, 128),))
    thickness = jnp.clip(jnp.exp(jax.random.uniform(keys[1], (LEV,), jnp.float32, math.log(0.1), math.log(0.4))), 0.1, 0.4)
    ocean_blocks = draw_ocean_blocks(jax.random.fold_in(keys[6], 71), 0)
    land_mask = draw_land_mask(jax.random.fold_in(keys[6], 71), 0)
    implicit_term = jnp.clip(jnp.exp(math.log(0.5) - 2.3025851 * jax.random.uniform(keys[4], (NY, NX), jnp.float32) ** shard_levels(keys[4], (NY, NX), ((0, 8), (1, 16)), -0.2, 0.2)), 0.05, 0.5)
    first_guess = centred(keys[5], (NY, NX), 1.0, 6.0, ((0, 8), (1, 16)), jnp.float32)
    return {"tendencies": tendencies, "thickness": thickness, "ocean_blocks": ocean_blocks, "land_mask": land_mask, "implicit_term": implicit_term, "first_guess": first_guess}


EAST_WEIGHT = 1.0
NORTH_WEIGHT = 1.0
CORNER_WEIGHT = 0.25
STENCIL_SUM = 5.0
LOWER_BOUND = 0.02
UPPER_BOUND = 2.0


def extend(operand):
    ghost_row = operand[-1:, ::-1]
    tall_field = jnp.concatenate([jnp.zeros_like(operand[:1]), operand, ghost_row], axis=0)
    return jnp.concatenate([tall_field[:, -1:], tall_field, tall_field[:, :1]], axis=1)


def operate(operand, ocean_mask, diagonal_total):
    padded = extend(operand)
    beside = EAST_WEIGHT * (padded[1:-1, 2:] + padded[1:-1, :-2])
    beside = beside + NORTH_WEIGHT * (padded[2:, 1:-1] + padded[:-2, 1:-1])
    beside = beside + CORNER_WEIGHT * ((padded[2:, 2:] + padded[2:, :-2]) + (padded[:-2, 2:] + padded[:-2, :-2]))
    return diagonal_total * operand - ocean_mask * beside


def line_factors(ocean_mask, diagonal_total, height):
    segments = ocean_mask.shape[0] // height
    columns = ocean_mask.shape[1]
    shaped_mask = ocean_mask.reshape(segments, height, columns)
    shaped_diag = diagonal_total.reshape(segments, height, columns)
    inverse_pivots = []
    ratios = []
    couplings = []
    for position in range(height):
        pivot_value = shaped_diag[:, position]
        if position > 0:
            pivot_value = pivot_value - couplings[position - 1] * ratios[position - 1]
        inverse = 1.0 / pivot_value
        if position + 1 < height:
            coupling = -NORTH_WEIGHT * shaped_mask[:, position] * shaped_mask[:, position + 1]
        else:
            coupling = jnp.zeros_like(pivot_value)
        couplings.append(coupling)
        ratios.append(coupling * inverse)
        inverse_pivots.append(inverse)
    return inverse_pivots, ratios, couplings


def line_solve(residual, factors, height):
    inverse_pivots, ratios, couplings = factors
    segments = residual.shape[0] // height
    columns = residual.shape[1]
    shaped = residual.reshape(segments, height, columns)
    forward = [shaped[:, 0] * inverse_pivots[0]]
    for position in range(1, height):
        forward.append((shaped[:, position] - couplings[position - 1] * forward[-1]) * inverse_pivots[position])
    backward = [forward[-1]]
    for position in range(height - 2, -1, -1):
        backward.append(forward[position] - ratios[position] * backward[-1])
    return jnp.stack(backward[::-1], axis=1).reshape(residual.shape)


def chebyshev_constants():
    alpha_value = 2.0 / (UPPER_BOUND - LOWER_BOUND)
    gamma_value = (UPPER_BOUND + LOWER_BOUND) / 2.0
    return gamma_value, 4.0 * alpha_value * alpha_value


def reference(tendencies, thickness, ocean_blocks, land_mask, implicit_term, first_guess):
    grid_rows, grid_cols = land_mask.shape
    block_rows = grid_rows // BY
    block_cols = grid_cols // BX
    column_sums = jnp.zeros((tendencies.shape[0], 2, BY, BX), jnp.float32)
    for layer_index in range(LEV):
        column_sums = column_sums + thickness[layer_index] * tendencies[:, :, layer_index].astype(jnp.float32)
    all_blocks = jnp.zeros((block_rows * block_cols, 2, BY, BX), jnp.float32).at[ocean_blocks].set(column_sums)
    forcing = all_blocks.reshape(block_rows, block_cols, 2, BY, BX).transpose(2, 0, 3, 1, 4).reshape(2, grid_rows, grid_cols)
    ocean_mask = land_mask.astype(jnp.float32)
    forcing = forcing * ocean_mask[None]
    zonal_padded = extend(forcing[0])
    meridional_padded = extend(forcing[1])
    right_side = ocean_mask * ((forcing[0] - zonal_padded[1:-1, :-2]) + (forcing[1] - meridional_padded[:-2, 1:-1]))
    diagonal_total = ocean_mask * (STENCIL_SUM + implicit_term) + (1.0 - ocean_mask)
    factors = line_factors(ocean_mask, diagonal_total, BY)
    solution = ocean_mask * first_guess
    residual = right_side - operate(solution, ocean_mask, diagonal_total)
    gamma_value, scale_value = chebyshev_constants()
    omega_value = 2.0 / gamma_value
    update = jnp.zeros_like(solution)
    for iteration in range(ITERS):
        smoothed = line_solve(residual, factors, BY)
        if iteration == 0:
            update = smoothed / gamma_value
        else:
            omega_value = 1.0 / (gamma_value - omega_value / scale_value)
            update = omega_value * smoothed + (gamma_value * omega_value - 1.0) * update
        solution = solution + update
        residual = residual - operate(update, ocean_mask, diagonal_total)
    padded = extend(solution)
    gradient = jnp.stack([ocean_mask * (padded[1:-1, 2:] - solution), ocean_mask * (padded[2:, 1:-1] - solution)])
    gradient_all = gradient.reshape(2, block_rows, BY, block_cols, BX).transpose(1, 3, 0, 2, 4).reshape(block_rows * block_cols, 2, BY, BX)
    return solution, residual, gradient_all[ocean_blocks]
```

```python
import functools

import jax
import jax.numpy as jnp
from jax import lax
from jax.experimental import pallas as pl
from jax.experimental.pallas import tpu as pltpu
from jax.sharding import PartitionSpec as P

BX = 128
BY = 16
BCOL = 4
BROW = 20
LEV = 24
ITERS = 4
STENCIL_SUM = 5.0
CORNER_WEIGHT = 0.25
LOWER_BOUND = 0.02
UPPER_BOUND = 2.0

F32 = jnp.float32
OWN = BROW + 4
EXT = 32
OFF = 8
DEPTH = 4
WIDE = BCOL * BX + BX
STRIP = DEPTH * BY + 8
BATCH = 8
VMEM_LIMIT = 48 << 20


def call(kernel, out_shape, operands, scratch=(), cost=1.0):
    spaces = [
        pl.BlockSpec(memory_space=pltpu.SMEM if a.dtype == jnp.int32 and a.ndim == 1 else pltpu.VMEM)
        for a in operands
    ]
    size = sum(a.size * a.dtype.itemsize for a in operands)
    return pl.pallas_call(
        kernel,
        out_shape=[jax.ShapeDtypeStruct(s, F32) for s in out_shape],
        in_specs=spaces,
        out_specs=[pl.BlockSpec(memory_space=pltpu.VMEM) for _ in out_shape],
        scratch_shapes=[pltpu.VMEM(s, F32) for s in scratch],
        compiler_params=pltpu.CompilerParams(vmem_limit_bytes=VMEM_LIMIT),
        cost_estimate=pl.CostEstimate(
            flops=int(cost * 4e6), bytes_accessed=int(size), transcendentals=0
        ),
    )(*operands)


def lanes(shape):
    return lax.broadcasted_iota(jnp.int32, shape, 1)


def rows(shape):
    return lax.broadcasted_iota(jnp.int32, shape, 0)


def pack(tiles, last):
    lane = lanes(tiles[0].shape)
    packed = jnp.zeros(tiles[0].shape, F32)
    for p, tile in enumerate(tiles):
        shift = (8 * p + 8 if last else 8 * p) % BX
        moved = pltpu.roll(tile, shift, 1) if shift else tile
        packed = jnp.where(lane // 8 == p, moved, packed)
    return packed


def unpack(packed, p, at):
    shift = (at - 8 * p) % BX
    return pltpu.roll(packed, shift, 1) if shift else packed


def side_tile(east, west, p):
    lane = lanes(east.shape)
    tile = jnp.where(lane < 8, unpack(east, p, 0), 0.0)
    return jnp.where(lane >= BX - 8, unpack(west, p, BX - 8), tile)


def turned(strip):
    lane = BX - 1 - lanes((strip.shape[0], BX))
    tiles = [strip[:, BX * q : BX * q + BX] for q in range(WIDE // BX)]
    tiles = [jnp.take_along_axis(tile, lane, axis=1) for tile in tiles]
    return jnp.concatenate([tiles[(BCOL - 1 - q) % (BCOL + 1)] for q in range(BCOL + 1)], axis=1)


def write_strips(flags, field, top_extra, bottom_extra, first, second, top, bottom, flipped):
    odd = flags[0] == 1
    for p in range(BY):
        top[DEPTH * p : DEPTH * p + DEPTH, :] = field[p, BROW - DEPTH : BROW, :]
        bottom[DEPTH * p : DEPTH * p + DEPTH, :] = field[p, 0:DEPTH, :]
    tail = DEPTH * BY
    first_row = rows((8, WIDE)) == 0
    top[tail:STRIP, :] = jnp.where(first_row, top_extra, 0.0)
    bottom[tail:STRIP, :] = jnp.where(first_row, bottom_extra, 0.0)
    first[...] = jnp.where(odd, bottom[...], top[...])

    @pl.when(flags[1] == 1)
    def _():
        for r in range(tail):
            flipped[r : r + 1, :] = top[tail - 1 - r : tail - r, :]
        flipped[tail:STRIP, :] = top[tail:STRIP, :]
        second[...] = turned(flipped[...])

    @pl.when(flags[1] == 0)
    def _():
        second[...] = jnp.where(odd, top[...], bottom[...])


def sums_kernel(dst, thickness, tendencies, out):
    step = pl.program_id(0)

    def block(n, carry):
        slot = dst[step * BATCH + n]
        for part in range(2):
            total = thickness[0] * tendencies[n, part, 0].astype(F32)
            for level in range(1, LEV):
                total = total + thickness[level] * tendencies[n, part, level].astype(F32)
            out[slot, part] = total
        return carry

    lax.fori_loop(0, BATCH, block, 0)


def prepare_kernel(mask, implicit, guess, diag, start, to_east, to_west, work):
    for q in range(BCOL):
        cols = slice(BX * q, BX * q + BX)
        m = mask[:, cols].astype(F32)
        work[q] = m * (STENCIL_SUM + implicit[:, cols]) + (1.0 - m)
        work[BCOL + q] = m * guess[:, cols]
    for k, field in enumerate((diag, start)):
        first, last = [], []
        for p in range(BY):
            for q in range(BCOL):
                tile = work[BCOL * k + q, pl.ds(p, BROW, stride=BY), :]
                tile = jnp.concatenate([tile, jnp.zeros((OWN - BROW, BX), F32)], axis=0)
                field[p, :, BX * q : BX * q + BX] = tile
                if q == 0:
                    first.append(tile)
                if q == BCOL - 1:
                    last.append(tile)
        to_east[OWN * k : OWN * k + OWN, :] = pack(last, True)
        to_west[OWN * k : OWN * k + OWN, :] = pack(first, False)


def widen_kernel(flags, diag, start, east, west, diag_wide, start_wide, first, second, *work):
    for k, (field, wide) in enumerate(((diag, diag_wide), (start, start_wide))):
        part = slice(OWN * k, OWN * k + OWN)
        for p in range(BY):
            wide[p, :, 0 : BCOL * BX] = field[p]
            wide[p, :, BCOL * BX : WIDE] = side_tile(east[part, :], west[part, :], p)
    write_strips(
        flags,
        diag_wide,
        start_wide[BY - 1, BROW - 1 : BROW, :],
        start_wide[0, 0:1, :],
        first,
        second,
        *work,
    )


def assemble(flags, field, first, second, out):
    odd = flags[0] == 1
    for p in range(BY):
        part = slice(DEPTH * p, DEPTH * p + DEPTH)
        out[p, 0 : OFF - DEPTH, :] = jnp.zeros((OFF - DEPTH, WIDE), F32)
        out[p, OFF - DEPTH : OFF, :] = jnp.where(odd, first[part, :], second[part, :])
        out[p, OFF : OFF + BROW, :] = field[p, 0:BROW, :]
        out[p, OFF + BROW : EXT, :] = jnp.where(odd, second[part, :], first[part, :])
    tail = DEPTH * BY
    north = jnp.where(odd, second[tail : tail + 1, :], first[tail : tail + 1, :])
    south = jnp.where(odd, first[tail : tail + 1, :], second[tail : tail + 1, :])
    return north, south


def beside(value):
    return pltpu.roll(value, 1, 1) + pltpu.roll(value, WIDE - 1, 1)


def factor_kernel(flags, diag, start, first, second, diag_full, inverse, start_full, minus_a, tall):
    north, south = assemble(flags, diag, first, second, diag_full)
    previous = jnp.zeros((EXT, WIDE), F32)
    for p in range(BY):
        d = diag_full[p]
        previous = jnp.where(d > 1.0, 1.0 / (d - previous), 0.0)
        inverse[p] = previous
    row = rows((EXT, WIDE))
    for p in range(BY):
        start_full[p, 0:OFF, :] = jnp.zeros((OFF, WIDE), F32)
        start_full[p, OFF:EXT, :] = start[p]
    start_full[0] = jnp.where(row == OFF + BROW, north, start_full[0])
    below = jnp.where(row == OFF - 1, south, start_full[BY - 1])
    for p in range(BY):
        x = start_full[p]
        tall[p] = x + CORNER_WEIGHT * beside(x)
    below = pltpu.roll(below + CORNER_WEIGHT * beside(below), 1, 0)
    for p in range(BY):
        x = start_full[p]
        south_part = tall[p - 1] if p > 0 else below
        north_part = tall[p + 1] if p + 1 < BY else pltpu.roll(tall[0], EXT - 1, 0)
        value = beside(x) + south_part + north_part - diag_full[p] * x
        minus_a[p] = value[OFF:EXT, 0 : BCOL * BX]


def place_kernel(loc, arrived, diag, minus_a, right, f1_top, to_east, to_west, work):
    def put(slot, carry):
        index = loc[slot]
        row, col = index >> 2, index & 3
        work[col, pl.ds(row, BY, stride=OWN), :] = arrived[slot, 0]
        work[BCOL + col, pl.ds(row, BY, stride=OWN), :] = arrived[slot, 1]
        return carry

    lax.fori_loop(0, arrived.shape[0], put, 0, unroll=8)
    lane = lanes((OWN, BX))
    row = rows((OWN, BX))
    first, last = [], []
    for q in range(BCOL):
        cols = slice(BX * q, BX * q + BX)

        def part(component, p, at):
            value = work[BCOL * component + at, OWN * p : OWN * p + OWN, :]
            return jnp.where(diag[p, :, BX * at : BX * at + BX] > 1.0, value, 0.0)

        south = jnp.where(row == 0, 0.0, pltpu.roll(part(1, BY - 1, q), 1, 0))
        for p in range(BY):
            f0 = part(0, p, q)
            f1 = part(1, p, q)
            west = pltpu.roll(f0, 1, 1)
            edge = pltpu.roll(part(0, p, q - 1), 1, 1) if q else 0.0
            west = jnp.where(lane == 0, edge, west)
            value = (f0 - west) + (f1 - south) + minus_a[p, :, cols]
            right[p, :, cols] = value
            south = f1
            if q == 0:
                first.append(value)
            if q == BCOL - 1:
                last.append(jnp.where(lane == BX - 5, pltpu.roll(f0, BX - 4, 1), value))
        f1_top[:, cols] = jnp.broadcast_to(south[BROW - 1 : BROW, :], (8, BX))
    to_west[...] = jnp.where(row == BROW, f1_top[0:1, 0:BX], pack(first, False))
    to_east[...] = jnp.where(row == BROW, f1_top[0:1, BX * (BCOL - 1) : BX * BCOL], pack(last, True))


def widen_right_kernel(flags, right, f1_top, mine, east, west, wide, f1_wide, first, second, *work):
    lane = lanes((OWN, BX))
    for p in range(BY):
        wide[p, :, BX : BCOL * BX] = right[p, :, BX:]
        wide[p, :, 0:BX] = right[p, :, 0:BX] - jnp.where(lane == 0, unpack(west[...], p, BX - 3), 0.0)
        tile = side_tile(east[...], west[...], p)
        wide[p, :, BCOL * BX : WIDE] = tile - jnp.where(lane == 0, unpack(mine[...], p, BX - 3), 0.0)
    f1_wide[:, 0 : BCOL * BX] = f1_top[...]
    lane = lanes((8, BX))
    tile = jnp.where(lane < 8, east[BROW : BROW + 1, :], 0.0)
    tile = jnp.where(lane >= BX - 8, west[BROW : BROW + 1, :], tile)
    f1_wide[:, BCOL * BX : WIDE] = tile
    write_strips(
        flags, wide, f1_wide[0:1, :], jnp.zeros((1, WIDE), F32), first, second, *work
    )


def solve_kernel(
    flags, loc, right, f1_wide, first, second, diag, inverse, start,
    solution, residual, slots,
    r_all, f_all, t_all, u_all, g_all, natural,
):
    north, south = assemble(flags, right, first, second, r_all)
    row = rows((EXT, WIDE))
    fold = jnp.where(flags[1] == 1, 0.0, 1.0)
    fix = jnp.where(row == OFF, south, 0.0)
    fix = fix + jnp.where(row == OFF + BROW, fold * f1_wide[0:1, :], 0.0)
    r_all[0] = r_all[0] - fix

    def gathered(p):
        below = t_all[p - 1] if p > 0 else pltpu.roll(t_all[BY - 1], 1, 0)
        above = t_all[p + 1] if p + 1 < BY else pltpu.roll(t_all[0], EXT - 1, 0)
        return r_all[p] + (below + above)

    gamma = (UPPER_BOUND + LOWER_BOUND) / 2.0
    alpha = 2.0 / (UPPER_BOUND - LOWER_BOUND)
    scale = 4.0 * alpha * alpha
    omega = 2.0 / gamma
    for k in range(ITERS):
        if k > 0:
            omega = 1.0 / (gamma - omega / scale)
        f = None
        for p in range(BY):
            if k > 0:
                r = gathered(p)
                r_all[p] = r
            else:
                r = r_all[p]
            f = (r if f is None else r + f) * inverse[p]
            f_all[p] = f
        s = None
        for p in reversed(range(BY)):
            s = f_all[p] if s is None else f_all[p] + inverse[p] * s
            if k == 0:
                u = s * (1.0 / gamma)
            else:
                u = omega * s + (gamma * omega - 1.0) * u_all[k - 1, p]
            u_all[k, p] = u
            h = beside(u)
            t_all[p] = u + CORNER_WEIGHT * h
            r_all[p] = r_all[p] + (h - diag[p] * u)
    for p in range(BY):
        r = jnp.where(diag[p] > 1.0, gathered(p), 0.0)
        x = start[p] + ((u_all[0, p] + u_all[1, p]) + (u_all[2, p] + u_all[3, p]))
        f_all[p] = x
        for q in range(BCOL):
            cols = slice(BX * q, BX * q + BX)
            natural[q, pl.ds(p, BROW, stride=BY), :] = x[OFF : OFF + BROW, cols]
            natural[BCOL + q, pl.ds(p, BROW, stride=BY), :] = r[OFF : OFF + BROW, cols]
    for q in range(BCOL):
        cols = slice(BX * q, BX * q + BX)
        solution[:, cols] = natural[q]
        residual[:, cols] = natural[BCOL + q]
    for p in range(BY):
        x = f_all[p]
        ocean = diag[p] > 1.0
        above = f_all[p + 1] if p + 1 < BY else pltpu.roll(f_all[0], EXT - 1, 0)
        zonal = jnp.where(ocean, pltpu.roll(x, WIDE - 1, 1) - x, 0.0)
        meridional = jnp.where(ocean, above - x, 0.0)
        for q in range(BCOL):
            cols = slice(BX * q, BX * q + BX)
            g_all[q, EXT * p : EXT * p + EXT, :] = zonal[:, cols]
            g_all[BCOL + q, EXT * p : EXT * p + EXT, :] = meridional[:, cols]

    def take(slot, carry):
        index = loc[slot]
        row, col = (index >> 2) + OFF, index & 3
        slots[slot, 0] = g_all[col, pl.ds(row, BY, stride=EXT), :]
        slots[slot, 1] = g_all[BCOL + col, pl.ds(row, BY, stride=EXT), :]
        return carry

    lax.fori_loop(0, slots.shape[0], take, 0, unroll=8)


def pick_kernel(dst, slots, out, sems):
    copies = [
        pltpu.make_async_copy(slots.at[dst[n]], out.at[n], sems.at[n]) for n in range(out.shape[0])
    ]
    for copy in copies:
        copy.start()
    for copy in copies:
        copy.wait()


def body(tendencies, thickness, ocean_blocks, land_mask, implicit_term, first_guess):
    nx = lax.axis_size("gx")
    ny = lax.axis_size("gy")
    gx = lax.axis_index("gx")
    gy = lax.axis_index("gy")
    devices = nx * ny
    listed = tendencies.shape[0]
    me = gx * ny + gy
    block_cols = BCOL * nx
    block_row = ocean_blocks // block_cols
    block_col = ocean_blocks % block_cols
    owner = block_col // BCOL * ny + block_row // BROW
    local = block_row % BROW * BCOL + block_col % BCOL
    dst = lax.dynamic_slice_in_dim(owner, me * listed, listed)
    loc = jnp.min(jnp.where(owner == me, local, BROW * BCOL).reshape(devices, listed), axis=1)
    flags = jnp.stack([gy % 2, (gy == ny - 1).astype(jnp.int32)]).astype(jnp.int32)

    east = [(i, (i + 1) % nx) for i in range(nx)]
    west = [(j, i) for i, j in east]
    swap_a, swap_b = [], []
    for i in range(nx):
        for j in range(ny):
            swap_a.append((i * ny + j, i * ny + (j ^ 1)))
            if j == ny - 1:
                swap_b.append((i * ny + j, (nx - 1 - i) * ny + j))
            elif j > 0:
                swap_b.append((i * ny + j, i * ny + (j + 1 if j % 2 else j - 1)))

    def exchange_x(to_east, to_west):
        return lax.ppermute(to_west, "gx", west), lax.ppermute(to_east, "gx", east)

    def exchange_y(first, second):
        return lax.ppermute(first, ("gx", "gy"), swap_a), lax.ppermute(second, ("gx", "gy"), swap_b)

    sums = pl.pallas_call(
        sums_kernel,
        grid_spec=pltpu.PrefetchScalarGridSpec(
            num_scalar_prefetch=2,
            grid=(listed // BATCH,),
            in_specs=[pl.BlockSpec((BATCH, 2, LEV, BY, BX), lambda i, *_: (i, 0, 0, 0, 0))],
            out_specs=pl.BlockSpec((devices, 2, BY, BX), lambda i, *_: (0, 0, 0, 0)),
        ),
        out_shape=jax.ShapeDtypeStruct((devices, 2, BY, BX), F32),
        compiler_params=pltpu.CompilerParams(vmem_limit_bytes=VMEM_LIMIT),
    )(dst, thickness, tendencies)
    arrived = lax.all_to_all(sums, ("gx", "gy"), split_axis=0, concat_axis=0, tiled=True)

    own = (BY, OWN, BCOL * BX)
    wide = (BY, OWN, WIDE)
    full = (BY, EXT, WIDE)
    strip = (STRIP, WIDE)
    diag, start, to_east, to_west = call(
        prepare_kernel,
        [own, own, (2 * OWN, BX), (2 * OWN, BX)],
        [land_mask, implicit_term, first_guess],
        [(2 * BCOL, BROW * BY, BX)],
    )
    diag, start, first, second = call(
        widen_kernel,
        [wide, wide, strip, strip],
        [flags, diag, start, *exchange_x(to_east, to_west)],
        [strip, strip, strip],
    )
    diag_full, inverse, start_full, minus_a = call(
        factor_kernel,
        [full, full, full, own],
        [flags, diag, start, *exchange_y(first, second)],
        [full],
    )
    right, f1_top, to_east, to_west = call(
        place_kernel,
        [own, (8, BCOL * BX), (OWN, BX), (OWN, BX)],
        [loc, arrived, diag, minus_a],
        [(2 * BCOL, BY * OWN, BX)],
    )
    right, f1_wide, first, second = call(
        widen_right_kernel,
        [wide, (8, WIDE), strip, strip],
        [flags, right, f1_top, to_east, *exchange_x(to_east, to_west)],
        [strip, strip, strip],
    )
    solution, residual, slots = call(
        solve_kernel,
        [(BROW * BY, BCOL * BX), (BROW * BY, BCOL * BX), (devices, 2, BY, BX)],
        [flags, loc, right, f1_wide, *exchange_y(first, second), diag_full, inverse, start_full],
        [
            full,
            full,
            full,
            (ITERS, *full),
            (2 * BCOL, BY * EXT, BX),
            (2 * BCOL, BROW * BY, BX),
        ],
        4.0,
    )
    returned = lax.all_to_all(slots, ("gx", "gy"), split_axis=0, concat_axis=0, tiled=True)
    gradient_blocks = pl.pallas_call(
        pick_kernel,
        out_shape=jax.ShapeDtypeStruct((listed, 2, BY, BX), F32),
        in_specs=[pl.BlockSpec(memory_space=pltpu.SMEM), pl.BlockSpec(memory_space=pl.ANY)],
        out_specs=pl.BlockSpec(memory_space=pl.ANY),
        scratch_shapes=[pltpu.SemaphoreType.DMA((listed,))],
    )(dst, returned)
    return solution, residual, gradient_blocks


def solution(mesh):
    placed = (
        P(("gx", "gy"), None, None, None, None),
        P(),
        P(),
        P("gy", "gx"),
        P("gy", "gx"),
        P("gy", "gx"),
    )
    return jax.shard_map(
        body,
        mesh=mesh,
        in_specs=placed,
        out_specs=(P("gy", "gx"), P("gy", "gx"), P(("gx", "gy"), None, None, None)),
        check_vma=False,
    )
```

```python
import functools

import jax
import jax.numpy as jnp
from jax import lax
from jax.experimental import pallas as pl
from jax.experimental.pallas import tpu as pltpu
from jax.sharding import PartitionSpec as P

BX = 128
BY = 16
BCOL = 4
BROW = 20
LEV = 24
ITERS = 4
STENCIL_SUM = 5.0
CORNER_WEIGHT = 0.25
LOWER_BOUND = 0.02
UPPER_BOUND = 2.0

F32 = jnp.float32
EXT = BROW + 4
OFF = 2
DEPTH = 2
WIDE = BCOL * BX + BX
PART = DEPTH * BY
STRIP = 2 * PART + 8
SENT = STRIP + 8
CHUNK = 4
MIB = 1 << 20
GAMMA = (UPPER_BOUND + LOWER_BOUND) / 2.0
SCALE = 4.0 * (2.0 / (UPPER_BOUND - LOWER_BOUND)) ** 2
OMEGAS = [2.0 / GAMMA]
for _ in range(1, ITERS):
    OMEGAS.append(1.0 / (GAMMA - OMEGAS[-1] / SCALE))


def call(kernel, out_shape, operands, scratch, vmem):
    spaces = [
        pl.BlockSpec(memory_space=pltpu.SMEM if a.dtype == jnp.int32 and a.ndim == 1 else pltpu.VMEM)
        for a in operands
    ]
    size = sum(a.size * a.dtype.itemsize for a in operands)
    return pl.pallas_call(
        kernel,
        out_shape=[jax.ShapeDtypeStruct(s, F32) for s in out_shape],
        in_specs=spaces,
        out_specs=[pl.BlockSpec(memory_space=pltpu.VMEM) for _ in out_shape],
        scratch_shapes=[pltpu.VMEM(s, F32) for s in scratch],
        compiler_params=pltpu.CompilerParams(vmem_limit_bytes=vmem * MIB),
        cost_estimate=pl.CostEstimate(flops=4000000, bytes_accessed=size, transcendentals=0),
    )(*operands)


def lanes(shape):
    return lax.broadcasted_iota(jnp.int32, shape, 1)


def rows(shape):
    return lax.broadcasted_iota(jnp.int32, shape, 0)


def pack(tiles, last):
    lane = lanes(tiles[0].shape)
    packed = jnp.zeros(tiles[0].shape, F32)
    for p, tile in enumerate(tiles):
        shift = (8 * p + 8 if last else 8 * p) % BX
        moved = pltpu.roll(tile, shift, 1) if shift else tile
        packed = jnp.where(lane // 8 == p, moved, packed)
    return packed


def unpack(packed, p, at):
    shift = (at - 8 * p) % BX
    return pltpu.roll(packed, shift, 1) if shift else packed


def side_tile(east, west, p):
    lane = lanes(east.shape)
    tile = jnp.where(lane < 8, unpack(east, p, 0), 0.0)
    return jnp.where(lane >= BX - 8, unpack(west, p, BX - 8), tile)


def turned(strip):
    lane = BX - 1 - lanes((strip.shape[0], BX))
    tiles = [strip[:, BX * q : BX * q + BX] for q in range(WIDE // BX)]
    tiles = [jnp.take_along_axis(tile, lane, axis=1) for tile in tiles]
    return jnp.concatenate([tiles[(BCOL - 1 - q) % (BCOL + 1)] for q in range(BCOL + 1)], axis=1)


def beside(value):
    return pltpu.roll(value, 1, 1) + pltpu.roll(value, WIDE - 1, 1)


def send(strip, message):
    message[0:STRIP, :] = strip[:, 0 : BCOL * BX]
    lane = lanes((8, BX))
    packed = [jnp.zeros((8, BX), F32) for _ in range(BCOL)]
    for g in range(STRIP // 8):
        tile = strip[8 * g : 8 * g + 8, BCOL * BX : WIDE]
        moved = pltpu.roll(tile, (8 + 16 * (g % 8)) % BX, 1)
        packed[g // 8] = jnp.where(lane // 16 == g % 8, moved, packed[g // 8])
    message[STRIP:SENT, :] = jnp.concatenate(packed, axis=1)


def receive(message, strip):
    strip[:, 0 : BCOL * BX] = message[0:STRIP, :]
    lane = lanes((8, BX))
    inside = (lane < 8) | (lane >= BX - 8)
    for g in range(STRIP // 8):
        tile = message[STRIP:SENT, BX * (g // 8) : BX * (g // 8) + BX]
        moved = pltpu.roll(tile, (BX - 8 - 16 * (g % 8)) % BX, 1)
        strip[8 * g : 8 * g + 8, BCOL * BX : WIDE] = jnp.where(inside, moved, 0.0)


def sums_kernel(thickness, blocks, tendencies, out, buffer, listed, staged, weights, sems, out_sems, list_sem):
    count = buffer.shape[0]
    ny = lax.axis_size("gy")
    me = lax.axis_index("gx") * ny + lax.axis_index("gy")
    listing = pltpu.make_async_copy(blocks, listed, list_sem)
    listing.start()

    def fetch(c):
        part = pl.ds(c * CHUNK, CHUNK)
        return pltpu.make_async_copy(tendencies.at[part], buffer.at[part], sems.at[c])

    def leave(n):
        index = listed[me * count + n]
        row, col = index // (BCOL * lax.axis_size("gx")), index % (BCOL * lax.axis_size("gx"))
        owner = col // BCOL * ny + row // BROW
        return pltpu.make_async_copy(staged.at[n], out.at[owner], out_sems.at[n])

    for c in range(count // CHUNK):
        fetch(c).start()
    for level in range(LEV):
        weights[level] = jnp.full((BY, BX), thickness[level], F32)
    listing.wait()

    def chunk(c, carry):
        fetch(c).wait()
        for pair in range(CHUNK // 2):
            totals = [None] * 4
            for level in range(LEV):
                weight = weights[level]
                for k in range(4):
                    n = c * CHUNK + 2 * pair + k // 2
                    term = weight * buffer[n, k % 2, level].astype(F32)
                    totals[k] = term if totals[k] is None else totals[k] + term
            for k in range(4):
                staged[c * CHUNK + 2 * pair + k // 2, k % 2] = totals[k]
            for k in range(2):
                leave(c * CHUNK + 2 * pair + k).start()
        return carry

    lax.fori_loop(0, count // CHUNK, chunk, 0)

    def finish(n, carry):
        leave(n).wait()
        return carry

    lax.fori_loop(0, count, finish, 0)


def prepare_kernel(mask, implicit, guess, fields, work):
    for q in range(BCOL):
        cols = slice(BX * q, BX * q + BX)
        m = mask[:, cols].astype(F32)
        work[q] = m * (STENCIL_SUM + implicit[:, cols]) + (1.0 - m)
        work[BCOL + q] = m * guess[:, cols]
    edge = jnp.zeros((OFF, BX), F32)
    for k in range(2):
        for p in range(BY):
            for q in range(BCOL):
                tile = work[BCOL * k + q, pl.ds(p, BROW, stride=BY), :]
                tile = jnp.concatenate([edge, tile, edge], axis=0)
                fields[k, p, :, BX * q : BX * q + BX] = tile


def place_kernel(loc, arrived, fields, right, f1_top, to_east, to_west, work):
    def put(slot, carry):
        index = loc[slot]
        row, col = (index >> 2) + OFF, index & 3
        work[col, pl.ds(row, BY, stride=EXT), :] = arrived[slot, 0]
        work[BCOL + col, pl.ds(row, BY, stride=EXT), :] = arrived[slot, 1]
        return carry

    lax.fori_loop(0, arrived.shape[0], put, 0, unroll=8)
    lane = lanes((EXT, BX))
    row = rows((EXT, BX))
    first, last = [], []
    for q in range(BCOL):
        cols = slice(BX * q, BX * q + BX)

        def part(component, p, at):
            value = work[BCOL * component + at, EXT * p : EXT * p + EXT, :]
            return jnp.where(fields[0, p, :, BX * at : BX * at + BX] > 1.0, value, 0.0)

        south = pltpu.roll(part(1, BY - 1, q), 1, 0)
        for p in range(BY):
            f0 = part(0, p, q)
            f1 = part(1, p, q)
            west = pltpu.roll(f0, 1, 1)
            edge = pltpu.roll(part(0, p, q - 1), 1, 1) if q else 0.0
            west = jnp.where(lane == 0, edge, west)
            value = (f0 - west) + (f1 - south)
            right[p, :, cols] = value
            south = f1
            if q == 0:
                first.append(value)
            if q == BCOL - 1:
                last.append(jnp.where(lane == BX - 5, pltpu.roll(f0, BX - 4, 1), value))
        f1_top[:, cols] = jnp.broadcast_to(south[OFF + BROW - 1 : OFF + BROW, :], (8, BX))
    f1_row = row == EXT - 1
    to_west[0:EXT, :] = jnp.where(f1_row, f1_top[0:1, 0:BX], pack(first, False))
    to_east[0:EXT, :] = jnp.where(f1_row, f1_top[0:1, BX * (BCOL - 1) : BX * BCOL], pack(last, True))
    for k in range(2):
        part_rows = slice(EXT * (k + 1), EXT * (k + 2))
        to_west[part_rows, :] = pack([fields[k, p, :, 0:BX] for p in range(BY)], False)
        to_east[part_rows, :] = pack([fields[k, p, :, BX * (BCOL - 1) :] for p in range(BY)], True)


def widen_kernel(
    flags, right, f1_top, mine, east, west, fields,
    r_wide, d_wide, x_wide, edges, first, second,
    tall, update, top, bottom, flipped,
):
    lane = lanes((EXT, BX))
    side = slice(BCOL * BX, WIDE)
    for k, wide in enumerate((d_wide, x_wide)):
        part = slice(EXT * (k + 1), EXT * (k + 2))
        for p in range(BY):
            wide[p, :, 0 : BCOL * BX] = fields[k, p]
            wide[p, :, side] = side_tile(east[part, :], west[part, :], p)
    for p in range(BY):
        x = x_wide[p]
        tall[p] = x + CORNER_WEIGHT * beside(x)
    for p in range(BY):
        below = tall[p - 1] if p > 0 else pltpu.roll(tall[BY - 1], 1, 0)
        above = tall[p + 1] if p + 1 < BY else pltpu.roll(tall[0], EXT - 1, 0)
        x = x_wide[p]
        minus = beside(x) + (below + above) - d_wide[p] * x
        r_wide[p, :, BX : BCOL * BX] = right[p, :, BX:] + minus[:, BX : BCOL * BX]
        fix = jnp.where(lane == 0, unpack(west[0:EXT, :], p, BX - 3), 0.0)
        r_wide[p, :, 0:BX] = right[p, :, 0:BX] - fix + minus[:, 0:BX]
        fix = jnp.where(lane == 0, unpack(mine[0:EXT, :], p, BX - 3), 0.0)
        r_wide[p, :, side] = side_tile(east[0:EXT, :], west[0:EXT, :], p) - fix + minus[:, side]
    lane = lanes((1, BX))
    tile = jnp.where(lane < 8, east[EXT - 1 : EXT, :], 0.0)
    tile = jnp.where(lane >= BX - 8, west[EXT - 1 : EXT, :], tile)
    f1 = jnp.concatenate([f1_top[0:1, :], tile], axis=1)
    t_top = tall[BY - 1, OFF + BROW - 1 : OFF + BROW, :]
    t_bottom = tall[0, OFF : OFF + 1, :]
    edges[0:1, :] = t_top - f1
    edges[1:2, :] = t_top
    edges[2:3, :] = t_bottom
    edges[3:8, :] = jnp.zeros((5, WIDE), F32)

    ends = (slice(0, 8), slice(EXT - 8, EXT))

    def ends_of(field, p):
        return jnp.concatenate([field[p, end, :] for end in ends], axis=0)

    def line(residual):
        lower = []
        for p in range(BY):
            lower.append(residual(p) * inverse[p] if p == 0 else (residual(p) + lower[-1]) * inverse[p])
        upper = [lower[-1]]
        for p in range(BY - 2, -1, -1):
            upper.append(lower[p] + inverse[p] * upper[-1])
        return upper[::-1]

    inverse = []
    for p in range(BY):
        d = ends_of(d_wide, p)
        inverse.append(jnp.where(d > 1.0, 1.0 / (d - inverse[-1] if p else d), 0.0))
    for p, s in enumerate(line(lambda p: ends_of(r_wide, p))):
        u = s * (1.0 / GAMMA)
        update[p] = u
        tall[p, 0:16, :] = u + CORNER_WEIGHT * beside(u)

    def after(p):
        below = tall[p - 1, 0:16, :] if p > 0 else pltpu.roll(tall[BY - 1, 0:16, :], 1, 0)
        above = tall[p + 1, 0:16, :] if p + 1 < BY else pltpu.roll(tall[0, 0:16, :], 15, 0)
        u = update[p]
        return ends_of(r_wide, p) + (beside(u) + (below + above) - ends_of(d_wide, p) * u)

    smoothed = line(after)
    behind = OFF + DEPTH, 16 - OFF - DEPTH - 1
    pick = [(0, behind[0], bottom), (BY - 1, behind[1], top)]
    for k, wide in enumerate((r_wide, d_wide)):
        for p in range(BY):
            rows_at = slice(PART * k + DEPTH * p, PART * k + DEPTH * p + DEPTH)
            top[rows_at, :] = wide[p, OFF + BROW - DEPTH : OFF + BROW, :]
            bottom[rows_at, :] = wide[p, OFF : OFF + DEPTH, :]
    at = 2 * PART
    for p, n, strip in pick:
        u = update[p, n : n + 1, :]
        strip[at : at + 1, :] = u
        strip[at + 1 : at + 2, :] = OMEGAS[1] * smoothed[p][n : n + 1, :] + (GAMMA * OMEGAS[1] - 1.0) * u
        strip[at + 4 : STRIP, :] = jnp.zeros((STRIP - at - 4, WIDE), F32)
    top[at + 2 : at + 3, :] = edges[0:1, :]
    top[at + 3 : at + 4, :] = x_wide[BY - 1, OFF + BROW - 1 : OFF + BROW, :]
    bottom[at + 2 : at + 3, :] = t_bottom
    bottom[at + 3 : at + 4, :] = x_wide[0, OFF : OFF + 1, :]

    @pl.when(flags[1] == 1)
    def _():
        for k in range(2):
            for r in range(PART):
                flipped[PART * k + r : PART * k + r + 1, :] = top[PART * (k + 1) - 1 - r : PART * (k + 1) - r, :]
        flipped[at:STRIP, :] = top[at:STRIP, :]
        flipped[at + 2 : at + 3, :] = edges[1:2, :]
        flipped[...] = turned(flipped[...])
        send(bottom, first)
        send(flipped, second)

    @pl.when((flags[0] == 1) & (flags[1] == 0))
    def _():
        send(bottom, first)
        send(top, second)

    @pl.when(flags[0] == 0)
    def _():
        send(top, first)
        send(bottom, second)


def solve_kernel(
    flags, loc, r_wide, d_wide, x_wide, edges, first, second,
    solution, residual, slots,
    r_all, d_all, inverse, f_all, t_all, u_all, g_all, natural, south, north,
):
    @pl.when(flags[0] == 1)
    def _():
        receive(first, south)
        receive(second, north)

    @pl.when(flags[0] == 0)
    def _():
        receive(second, south)
        receive(first, north)

    row = rows((EXT, WIDE))
    previous = jnp.zeros((EXT, WIDE), F32)
    for k, (field, out) in enumerate(((r_wide, r_all), (d_wide, d_all))):
        for p in range(BY):
            part = slice(PART * k + DEPTH * p, PART * k + DEPTH * p + DEPTH)
            out[p] = field[p]
            out[p, 0:OFF, :] = south[part, :]
            out[p, OFF + BROW : EXT, :] = north[part, :]
    for p in range(BY):
        d = d_all[p]
        previous = jnp.where(d > 1.0, 1.0 / (d - previous), 0.0)
        inverse[p] = previous
    at = 2 * PART
    upward = jnp.where(flags[1] == 1, edges[1:2, :], edges[0:1, :])
    fix = jnp.where(row == OFF, south[at + 2 : at + 3, :], 0.0)
    r_all[0] = r_all[0] + jnp.where(row == OFF + BROW, upward, fix)
    fix = jnp.where(row == OFF + BROW - 1, north[at + 2 : at + 3, :], 0.0)
    r_all[BY - 1] = r_all[BY - 1] + jnp.where(row == OFF - 1, edges[2:3, :], fix)

    def gathered(p, k):
        below = t_all[p - 1] if p > 0 else pltpu.roll(t_all[BY - 1], 1, 0)
        above = t_all[p + 1] if p + 1 < BY else pltpu.roll(t_all[0], EXT - 1, 0)
        if k <= 2:
            at_k = slice(at + k - 1, at + k)
            if p == 0:
                u = south[at_k, :]
                below = jnp.where(row == 0, u + CORNER_WEIGHT * beside(u), below)
            if p == BY - 1:
                u = north[at_k, :]
                above = jnp.where(row == EXT - 1, u + CORNER_WEIGHT * beside(u), above)
        return r_all[p] + (below + above)

    for k, omega in enumerate(OMEGAS):
        f = None
        for p in range(BY):
            if k > 0:
                r = gathered(p, k)
                r_all[p] = r
            else:
                r = r_all[p]
            f = (r if f is None else r + f) * inverse[p]
            f_all[p] = f
        s = None
        for p in reversed(range(BY)):
            s = f_all[p] if s is None else f_all[p] + inverse[p] * s
            if k == 0:
                u = s * (1.0 / GAMMA)
            else:
                u = omega * s + (GAMMA * omega - 1.0) * u_all[k - 1, p]
            u_all[k, p] = u
            h = beside(u)
            t_all[p] = u + CORNER_WEIGHT * h
            r_all[p] = r_all[p] + (h - d_all[p] * u)
    for p in range(BY):
        r = jnp.where(d_all[p] > 1.0, gathered(p, ITERS), 0.0)
        start = x_wide[p]
        if p == 0:
            start = jnp.where(row == OFF + BROW, north[at + 3 : at + 4, :], start)
        x = start + ((u_all[0, p] + u_all[1, p]) + (u_all[2, p] + u_all[3, p]))
        f_all[p] = x
        for q in range(BCOL):
            cols = slice(BX * q, BX * q + BX)
            natural[q, pl.ds(p, BROW, stride=BY), :] = x[OFF : OFF + BROW, cols]
            natural[BCOL + q, pl.ds(p, BROW, stride=BY), :] = r[OFF : OFF + BROW, cols]
    for q in range(BCOL):
        cols = slice(BX * q, BX * q + BX)
        solution[:, cols] = natural[q]
        residual[:, cols] = natural[BCOL + q]
    for p in range(BY):
        x = f_all[p]
        ocean = d_all[p] > 1.0
        above = f_all[p + 1] if p + 1 < BY else pltpu.roll(f_all[0], EXT - 1, 0)
        zonal = jnp.where(ocean, pltpu.roll(x, WIDE - 1, 1) - x, 0.0)
        meridional = jnp.where(ocean, above - x, 0.0)
        for q in range(BCOL):
            cols = slice(BX * q, BX * q + BX)
            g_all[q, EXT * p : EXT * p + EXT, :] = zonal[:, cols]
            g_all[BCOL + q, EXT * p : EXT * p + EXT, :] = meridional[:, cols]

    def take(slot, carry):
        index = loc[slot]
        row, col = (index >> 2) + OFF, index & 3
        slots[slot, 0] = g_all[col, pl.ds(row, BY, stride=EXT), :]
        slots[slot, 1] = g_all[BCOL + col, pl.ds(row, BY, stride=EXT), :]
        return carry

    lax.fori_loop(0, slots.shape[0], take, 0, unroll=8)


def pick_kernel(dst, slots, out, sems):
    copies = [
        pltpu.make_async_copy(slots.at[dst[n]], out.at[n], sems.at[n]) for n in range(out.shape[0])
    ]
    for copy in copies:
        copy.start()
    for copy in copies:
        copy.wait()


def body(tendencies, thickness, ocean_blocks, land_mask, implicit_term, first_guess):
    nx = lax.axis_size("gx")
    ny = lax.axis_size("gy")
    gx = lax.axis_index("gx")
    gy = lax.axis_index("gy")
    devices = nx * ny
    listed = tendencies.shape[0]
    me = gx * ny + gy
    block_cols = BCOL * nx
    block_row = ocean_blocks // block_cols
    block_col = ocean_blocks % block_cols
    owner = block_col // BCOL * ny + block_row // BROW
    local = block_row % BROW * BCOL + block_col % BCOL
    dst = lax.dynamic_slice_in_dim(owner, me * listed, listed)
    loc = jnp.min(jnp.where(owner == me, local, BROW * BCOL).reshape(devices, listed), axis=1)
    flags = jnp.stack([gy % 2, (gy == ny - 1).astype(jnp.int32)]).astype(jnp.int32)

    east = [(i, (i + 1) % nx) for i in range(nx)]
    west = [(j, i) for i, j in east]
    swap_a, swap_b = [], []
    for i in range(nx):
        for j in range(ny):
            swap_a.append((i * ny + j, i * ny + (j ^ 1)))
            if j == ny - 1:
                swap_b.append((i * ny + j, (nx - 1 - i) * ny + j))
            elif j > 0:
                swap_b.append((i * ny + j, i * ny + (j + 1 if j % 2 else j - 1)))

    def exchange_x(to_east, to_west):
        return lax.ppermute(to_west, "gx", west), lax.ppermute(to_east, "gx", east)

    def exchange_y(first, second):
        return lax.ppermute(first, ("gx", "gy"), swap_a), lax.ppermute(second, ("gx", "gy"), swap_b)

    hbm = pl.BlockSpec(memory_space=pltpu.HBM)
    sums = pl.pallas_call(
        sums_kernel,
        out_shape=jax.ShapeDtypeStruct((devices, 2, BY, BX), F32),
        in_specs=[pl.BlockSpec(memory_space=pltpu.SMEM), hbm, hbm],
        out_specs=hbm,
        scratch_shapes=[
            pltpu.VMEM(tendencies.shape, tendencies.dtype),
            pltpu.SMEM(ocean_blocks.shape, jnp.int32),
            pltpu.VMEM((listed, 2, BY, BX), F32),
            pltpu.VMEM((LEV, BY, BX), F32),
            pltpu.SemaphoreType.DMA((listed // CHUNK,)),
            pltpu.SemaphoreType.DMA((listed,)),
            pltpu.SemaphoreType.DMA,
        ],
        compiler_params=pltpu.CompilerParams(vmem_limit_bytes=58 * MIB),
    )(thickness, ocean_blocks, tendencies)
    arrived = lax.all_to_all(sums, ("gx", "gy"), split_axis=0, concat_axis=0, tiled=True)

    own = (BY, EXT, BCOL * BX)
    full = (BY, EXT, WIDE)
    strip = (STRIP, WIDE)
    sent = (SENT, BCOL * BX)
    sums, land_mask, implicit_term, first_guess = lax.optimization_barrier(
        (sums, land_mask, implicit_term, first_guess)
    )
    (fields,) = call(
        prepare_kernel,
        [(2, *own)],
        [land_mask, implicit_term, first_guess],
        [(2 * BCOL, BROW * BY, BX)],
        6,
    )
    right, f1_top, to_east, to_west = call(
        place_kernel,
        [own, (8, BCOL * BX), (3 * EXT, BX), (3 * EXT, BX)],
        [loc, arrived, fields],
        [(2 * BCOL, BY * EXT, BX)],
        8,
    )
    r_wide, d_wide, x_wide, edges, first, second = call(
        widen_kernel,
        [full, full, full, (8, WIDE), sent, sent],
        [flags, right, f1_top, to_east, *exchange_x(to_east, to_west), fields],
        [full, (BY, 16, WIDE), strip, strip, strip],
        12,
    )
    solution, residual, slots = call(
        solve_kernel,
        [(BROW * BY, BCOL * BX), (BROW * BY, BCOL * BX), (devices, 2, BY, BX)],
        [flags, loc, r_wide, d_wide, x_wide, edges, *exchange_y(first, second)],
        [
            full,
            full,
            full,
            full,
            full,
            (ITERS, *full),
            (2 * BCOL, BY * EXT, BX),
            (2 * BCOL, BROW * BY, BX),
            strip,
            strip,
        ],
        20,
    )
    returned = lax.all_to_all(slots, ("gx", "gy"), split_axis=0, concat_axis=0, tiled=True)
    gradient_blocks = pl.pallas_call(
        pick_kernel,
        out_shape=jax.ShapeDtypeStruct((listed, 2, BY, BX), F32),
        in_specs=[pl.BlockSpec(memory_space=pltpu.SMEM), pl.BlockSpec(memory_space=pltpu.VMEM)],
        out_specs=pl.BlockSpec(memory_space=pl.ANY),
        scratch_shapes=[pltpu.SemaphoreType.DMA((listed,))],
        compiler_params=pltpu.CompilerParams(vmem_limit_bytes=4 * MIB),
    )(dst, returned)
    return solution, residual, gradient_blocks


def solution(mesh):
    placed = (
        P(("gx", "gy"), None, None, None, None),
        P(),
        P(),
        P("gy", "gx"),
        P("gy", "gx"),
        P("gy", "gx"),
    )
    return jax.shard_map(
        body,
        mesh=mesh,
        in_specs=placed,
        out_specs=(P("gy", "gx"), P("gy", "gx"), P(("gx", "gy"), None, None, None)),
        check_vma=False,
    )
```

```python
import functools

import jax
import jax.numpy as jnp
from jax import lax
from jax.experimental import pallas as pl
from jax.experimental.pallas import tpu as pltpu
from jax.sharding import PartitionSpec as P

BX = 128
BY = 16
BCOL = 4
BROW = 20
LEV = 24
ITERS = 4
STENCIL_SUM = 5.0
CORNER_WEIGHT = 0.25
LOWER_BOUND = 0.02
UPPER_BOUND = 2.0

F32 = jnp.float32
EXT = BROW + 4
OFF = 2
DEPTH = 1
WIDE = BCOL * BX + BX
PART = DEPTH * BY
SINGLE = 6
STRIP = 2 * PART + 8
SENT = STRIP
CHUNK = 4
MIB = 1 << 20
GAMMA = (UPPER_BOUND + LOWER_BOUND) / 2.0
SCALE = 4.0 * (2.0 / (UPPER_BOUND - LOWER_BOUND)) ** 2
OMEGAS = [2.0 / GAMMA]
for _ in range(1, ITERS):
    OMEGAS.append(1.0 / (GAMMA - OMEGAS[-1] / SCALE))


def call(kernel, out_shape, operands, scratch, vmem):
    spaces = [
        pl.BlockSpec(memory_space=pltpu.SMEM if a.dtype == jnp.int32 and a.ndim == 1 else pltpu.VMEM)
        for a in operands
    ]
    return pl.pallas_call(
        kernel,
        out_shape=[jax.ShapeDtypeStruct(s, F32) for s in out_shape],
        in_specs=spaces,
        out_specs=[pl.BlockSpec(memory_space=pltpu.VMEM) for _ in out_shape],
        scratch_shapes=[pltpu.VMEM(s, F32) for s in scratch],
        compiler_params=pltpu.CompilerParams(vmem_limit_bytes=vmem * MIB),
        cost_estimate=pl.CostEstimate(flops=1, bytes_accessed=1, transcendentals=0),
    )(*operands)


def lanes(shape):
    return lax.broadcasted_iota(jnp.int32, shape, 1)


def rows(shape):
    return lax.broadcasted_iota(jnp.int32, shape, 0)


def pack(tiles, last):
    lane = lanes(tiles[0].shape)
    packed = jnp.zeros(tiles[0].shape, F32)
    for p, tile in enumerate(tiles):
        shift = (8 * p + 8 if last else 8 * p) % BX
        moved = pltpu.roll(tile, shift, 1) if shift else tile
        packed = jnp.where(lane // 8 == p, moved, packed)
    return packed


def unpack(packed, p, at):
    shift = (at - 8 * p) % BX
    return pltpu.roll(packed, shift, 1) if shift else packed


def side_tile(east, west, p):
    lane = lanes(east.shape)
    tile = jnp.where(lane < 8, unpack(east, p, 0), 0.0)
    return jnp.where(lane >= BX - 8, unpack(west, p, BX - 8), tile)


def turned(strip):
    lane = BX - 1 - lanes((strip.shape[0], BX))
    tiles = [strip[:, BX * q : BX * q + BX] for q in range(WIDE // BX)]
    tiles = [jnp.take_along_axis(tile, lane, axis=1) for tile in tiles]
    return jnp.concatenate([tiles[(BCOL - 1 - q) % (BCOL + 1)] for q in range(BCOL + 1)], axis=1)


def beside(value):
    return pltpu.roll(value, 1, 1) + pltpu.roll(value, WIDE - 1, 1)


def send(strip, message):
    message[0 : 2 * PART, :] = strip[0 : 2 * PART, 0 : BCOL * BX]
    lane = lanes((8, BX))
    packed = jnp.zeros((8, BX), F32)
    for g in range(STRIP // 8):
        tile = strip[8 * g : 8 * g + 8, BCOL * BX : WIDE]
        packed = jnp.where(lane // 16 == g, pltpu.roll(tile, (8 + 16 * g) % BX, 1), packed)
    message[2 * PART : SENT, 0:BX] = packed
    for k in range(SINGLE):
        for q in range(BCOL):
            n = BCOL * k + q
            cols = slice(BX * (1 + n // 8), BX * (2 + n // 8))
            message[2 * PART + n % 8 : 2 * PART + n % 8 + 1, cols] = strip[
                2 * PART + k : 2 * PART + k + 1, BX * q : BX * q + BX
            ]


def receive(message, strip):
    strip[0 : 2 * PART, 0 : BCOL * BX] = message[0 : 2 * PART, :]
    lane = lanes((8, BX))
    inside = (lane < 8) | (lane >= BX - 8)
    packed = message[2 * PART : SENT, 0:BX]
    for g in range(STRIP // 8):
        moved = pltpu.roll(packed, (BX - 8 - 16 * g) % BX, 1)
        strip[8 * g : 8 * g + 8, BCOL * BX : WIDE] = jnp.where(inside, moved, 0.0)
    for k in range(SINGLE):
        for q in range(BCOL):
            n = BCOL * k + q
            cols = slice(BX * (1 + n // 8), BX * (2 + n // 8))
            strip[2 * PART + k : 2 * PART + k + 1, BX * q : BX * q + BX] = message[
                2 * PART + n % 8 : 2 * PART + n % 8 + 1, cols
            ]


def sums_kernel(
    thickness, blocks, tendencies, out, buffer, listed, staged, edges, weights, sems, out_sems, other_sems
):
    count = buffer.shape[0]
    nx, ny = lax.axis_size("gx"), lax.axis_size("gy")
    me = lax.axis_index("gx") * ny + lax.axis_index("gy")
    listing = pltpu.make_async_copy(blocks, listed, other_sems.at[0])
    listing.start()

    def fetch(c):
        part = pl.ds(c * CHUNK, CHUNK)
        return pltpu.make_async_copy(tendencies.at[part], buffer.at[part], sems.at[c])

    def leave(n, owner):
        return pltpu.make_async_copy(staged.at[n], out.at[owner, pl.ds(0, 2 * BY // 4)], out_sems.at[n])

    row16, lane16 = rows((BY, BX)), lanes((BY, BX))
    row4 = rows((4, BX))

    for c in range(count // CHUNK):
        fetch(c).start()
    for level in range(LEV):
        weights[level] = jnp.full((BY, BX), thickness[level], F32)
    listing.wait()

    def chunk(c, carry):
        fetch(c).wait()
        for pair in range(CHUNK // 2):
            totals = [None] * 4
            for level in range(LEV):
                weight = weights[level]
                for k in range(4):
                    n = c * CHUNK + 2 * pair + k // 2
                    term = weight * buffer[n, k % 2, level].astype(F32)
                    totals[k] = term if totals[k] is None else totals[k] + term
            for k in range(2):
                n = c * CHUNK + 2 * pair + k
                index = listed[me * count + n]
                row, col = lax.div(index, BCOL * nx), lax.rem(index, BCOL * nx)
                tile_row, tile_col, at = lax.div(row, BROW), lax.div(col, BCOL), lax.rem(col, BCOL)
                both = totals[2 * k : 2 * k + 2]
                for part in range(2):
                    staged[n, 4 * part : 4 * part + 4] = both[part].reshape(4, 4, BX)
                leave(n, tile_col * ny + tile_row).start()
                east_edge = at == BCOL - 1
                source = lane16 % 8 + jnp.where(east_edge, BX - 8, 0)
                line = []
                for value in both:
                    spread = jnp.take_along_axis(value, source, axis=1)
                    spread = jnp.where(lane16 // 8 == row16, spread, 0.0)
                    line.append(jnp.sum(spread, axis=0, keepdims=True))
                beside_col = lax.rem(tile_col + jnp.where(east_edge, 1, nx - 1), nx)
                slot = jnp.where((at == 0) | east_edge, beside_col * ny + tile_row, edges.shape[0] - 1)
                value = jnp.where(row4 % 2 == 0, line[0], line[1])
                edges[slot] = jnp.where(row4 // 2 == jnp.where(east_edge, 1, 0), value, edges[slot])
        return carry

    lax.fori_loop(0, count // CHUNK, chunk, 0)
    sides = pltpu.make_async_copy(edges.at[pl.ds(0, nx * ny)], out.at[:, 2 * BY // 4], other_sems.at[1])
    sides.start()

    def finish(n, carry):
        leave(n, 0).wait()
        return carry

    lax.fori_loop(0, count, finish, 0)
    sides.wait()


def prepare_kernel(mask, implicit, guess, fields, to_east, to_west, work):
    for q in range(BCOL):
        cols = slice(BX * q, BX * q + BX)
        m = mask[:, cols].astype(F32)
        work[q] = m * (STENCIL_SUM + implicit[:, cols]) + (1.0 - m)
        work[BCOL + q] = m * guess[:, cols]
    edge = jnp.zeros((OFF, BX), F32)
    for k in range(2):
        for p in range(BY):
            for q in range(BCOL):
                tile = work[BCOL * k + q, pl.ds(p, BROW, stride=BY), :]
                tile = jnp.concatenate([edge, tile, edge], axis=0)
                fields[k, p, :, BX * q : BX * q + BX] = tile
        part = slice(EXT * k, EXT * k + EXT)
        to_west[part, :] = pack([fields[k, p, :, 0:BX] for p in range(BY)], False)
        to_east[part, :] = pack([fields[k, p, :, BX * (BCOL - 1) :] for p in range(BY)], True)


def put_blocks(came, arrived, work, first_row, count, height, offset):
    row16, lane16 = rows((BY, BX)), lanes((BY, BX))
    spread = 8 * row16 + lane16 % 8

    def put(n, carry):
        block_row = jnp.clip(first_row + n, 0, BROW - 1)
        at_rows = pl.ds(n + offset, BY, stride=height)
        for col in range(BCOL):
            slot = came[block_row * BCOL + col]
            for part in range(2):
                value = arrived[slot, 4 * part : 4 * part + 4].reshape(BY, BX)
                work[(BCOL + 2) * part + col, at_rows, :] = value
        for side in range(2):
            slot = came[(BCOL + side) * BROW + block_row]
            for part in range(2):
                line = arrived[slot, 8, 2 * side + part : 2 * side + part + 1]
                value = jnp.take_along_axis(jnp.broadcast_to(line, (BY, BX)), spread, axis=1)
                work[(BCOL + 2) * part + BCOL + side, at_rows, :] = value
        return carry

    lax.fori_loop(0, count, put, 0, unroll=4)


def right_side(work, fields, east, west, parts, r_wide, d_wide, x_wide, inverse, tall):
    height = sum(high - low for low, high in parts)
    for k, wide in enumerate((d_wide, x_wide)):
        sides = [
            jnp.concatenate([side[EXT * k + low : EXT * k + high, :] for low, high in parts], axis=0)
            for side in (east, west)
        ]
        for p in range(BY):
            at = 0
            for low, high in parts:
                wide[p, at : at + high - low, 0 : BCOL * BX] = fields[k, p, low:high, :]
                at += high - low
            wide[p, :, BCOL * BX : WIDE] = side_tile(*sides, p)
    previous = None
    for p in range(BY):
        d = d_wide[p]
        previous = jnp.where(d > 1.0, 1.0 / (d if p == 0 else d - previous), 0.0)
        inverse[p] = previous
        x = x_wide[p]
        tall[p] = x + CORNER_WEIGHT * beside(x)
    lane = lanes((height, BX))

    def forcing(part, p):
        at = slice(height * p, height * p + height)
        tiles = [work[(BCOL + 2) * part + q, at, :] for q in range(BCOL + 2)]
        tiles[BCOL] = jnp.where(lane < BX // 2, tiles[BCOL], tiles[BCOL + 1])
        value = jnp.concatenate(tiles[: BCOL + 1], axis=1)
        return jnp.where(d_wide[p] > 1.0, value, 0.0)

    last = forcing(1, BY - 1)
    south = pltpu.roll(last, 1, 0)
    for p in range(BY):
        f0 = forcing(0, p)
        f1 = forcing(1, p) if p + 1 < BY else last
        below = tall[p - 1] if p > 0 else pltpu.roll(tall[BY - 1], 1, 0)
        above = tall[p + 1] if p + 1 < BY else pltpu.roll(tall[0], height - 1, 0)
        x = x_wide[p]
        minus_a = beside(x) + (below + above) - d_wide[p] * x
        r_wide[p] = (f0 - pltpu.roll(f0, 1, 1)) + (f1 - south) + minus_a
        south = f1
    return last


def right_kernel(
    came, arrived, fields, east, west,
    r_wide, d_wide, x_wide, inverse, edges,
    work, tall,
):
    put_blocks(came, arrived, work, 0, BROW, EXT, OFF)
    last = right_side(work, fields, east, west, ((0, EXT),), r_wide, d_wide, x_wide, inverse, tall)
    t_top = tall[BY - 1, OFF + BROW - 1 : OFF + BROW, :]
    edges[0:1, :] = t_top - last[OFF + BROW - 1 : OFF + BROW, :]
    edges[1:2, :] = t_top
    edges[2:3, :] = tall[0, OFF : OFF + 1, :]
    edges[3:8, :] = jnp.zeros((5, WIDE), F32)


def ends_kernel(
    flags, came, arrived, fields, east, west, first, second,
    work, r_wide, d_wide, x_wide, inverse, tall, update, top, bottom, flipped,
):
    put_blocks(came, arrived, work, -OFF, 8, 16, 0)
    put_blocks(came, arrived, work, EXT - 8 - OFF, 8, 16, 8)
    parts = ((0, 8), (EXT - 8, EXT))
    last = right_side(work, fields, east, west, parts, r_wide, d_wide, x_wide, inverse, tall)
    at = 2 * PART
    south, north = OFF, 16 - OFF - 1
    for k, wide in enumerate((r_wide, d_wide)):
        for p in range(BY):
            part = slice(PART * k + DEPTH * p, PART * k + DEPTH * p + DEPTH)
            top[part, :] = wide[p, north : north + DEPTH, :]
            bottom[part, :] = wide[p, south : south + DEPTH, :]
    t_top = tall[BY - 1, north : north + 1, :]
    top[at + 4 : at + 5, :] = t_top - jnp.where(flags[1] == 1, 0.0, last[north : north + 1, :])
    top[at + 5 : at + 6, :] = x_wide[BY - 1, north : north + 1, :]
    bottom[at + 4 : at + 5, :] = tall[0, south : south + 1, :]
    bottom[at + 5 : at + 6, :] = x_wide[0, south : south + 1, :]

    def line():
        lower = []
        for p in range(BY):
            r = r_wide[p] if p == 0 else r_wide[p] + lower[-1]
            lower.append(r * inverse[p])
        upper = [lower[-1]]
        for p in range(BY - 2, -1, -1):
            upper.append(lower[p] + inverse[p] * upper[-1])
        return upper[::-1]

    behind = ((0, south + 1, bottom), (BY - 1, north - 1, top))
    row = rows((16, WIDE))
    strips = (row == south) | (row == north)
    for k in range(2):
        for p, s in enumerate(line()):
            u = s * (1.0 / GAMMA) if k == 0 else OMEGAS[1] * s + (GAMMA * OMEGAS[1] - 1.0) * update[p]
            update[p] = u
            t = u + CORNER_WEIGHT * beside(u)
            tall[p] = t if k == 0 else jnp.where(strips, 0.0, t)
        for p in range(BY):
            below = tall[p - 1] if p > 0 else pltpu.roll(tall[BY - 1], 1, 0)
            above = tall[p + 1] if p + 1 < BY else pltpu.roll(tall[0], 15, 0)
            u = update[p]
            r_wide[p] = r_wide[p] + (beside(u) + (below + above) - d_wide[p] * u)
        for p, n, strip in behind:
            strip[at + k : at + k + 1, :] = update[p, n : n + 1, :]
    smoothed = line()
    element = None
    for p in reversed(range(BY)):
        d = d_wide[p]
        element = jnp.where(d > 1.0, 1.0 / (d if element is None else d - element), 0.0)
    for (p, n, strip), diagonal in zip(behind, (element, inverse[BY - 1])):
        strip[at + 2 : at + 3, :] = smoothed[p][n : n + 1, :]
        strip[at + 3 : at + 4, :] = diagonal[n : n + 1, :]
        strip[at + SINGLE : STRIP, :] = jnp.zeros((STRIP - at - SINGLE, WIDE), F32)

    @pl.when(flags[1] == 1)
    def _():
        for k in range(2):
            for r in range(PART):
                flipped[PART * k + r : PART * k + r + 1, :] = top[PART * (k + 1) - 1 - r : PART * (k + 1) - r, :]
        flipped[at:STRIP, :] = top[at:STRIP, :]
        top[...] = turned(flipped[...])

    @pl.when(flags[0] == 1)
    def _():
        send(bottom, first)
        send(top, second)

    @pl.when(flags[0] == 0)
    def _():
        send(top, first)
        send(bottom, second)


def solve_kernel(
    flags, loc, r_wide, d_wide, x_wide, inverse_own, edges, first, second,
    solution, residual, slots,
    r_all, d_all, inverse, f_all, t_all, u_all, g_all, natural, south, north, sems,
):
    @pl.when(flags[0] == 1)
    def _():
        receive(first, south)
        receive(second, north)

    @pl.when(flags[0] == 0)
    def _():
        receive(second, south)
        receive(first, north)

    row = rows((EXT, WIDE))
    for k, (field, out) in enumerate(((r_wide, r_all), (d_wide, d_all))):
        for p in range(BY):
            part = slice(PART * k + DEPTH * p, PART * k + DEPTH * p + DEPTH)
            out[p] = field[p]
            out[p, OFF - DEPTH : OFF, :] = south[part, :]
            out[p, OFF + BROW : OFF + BROW + DEPTH, :] = north[part, :]
    previous = None
    for p in range(BY):
        d = jnp.concatenate([d_all[p, 0:8, :], d_all[p, EXT - 8 : EXT, :]], axis=0)
        previous = jnp.where(d > 1.0, 1.0 / (d if p == 0 else d - previous), 0.0)
        inverse[p, 0:8, :] = previous[0:8, :]
        inverse[p, 8 : EXT - 8, :] = inverse_own[p, 8 : EXT - 8, :]
        inverse[p, EXT - 8 : EXT, :] = previous[8:16, :]
    at = 2 * PART
    upward = jnp.where(flags[1] == 1, edges[1:2, :], edges[0:1, :])
    fix = jnp.where(row == OFF, south[at + 4 : at + 5, :], 0.0)
    r_all[0] = r_all[0] + jnp.where(row == OFF + BROW, upward, fix)
    fix = jnp.where(row == OFF + BROW - 1, north[at + 4 : at + 5, :], 0.0)
    r_all[BY - 1] = r_all[BY - 1] + jnp.where(row == OFF - 1, edges[2:3, :], fix)

    def gathered(p, k):
        below = t_all[p - 1] if p > 0 else pltpu.roll(t_all[BY - 1], 1, 0)
        above = t_all[p + 1] if p + 1 < BY else pltpu.roll(t_all[0], EXT - 1, 0)
        if k < ITERS:
            at_k = slice(at + k - 1, at + k)
            if p == 0:
                u = south[at_k, :]
                below = jnp.where(row == OFF - 1, u + CORNER_WEIGHT * beside(u), below)
            if p == BY - 1:
                u = north[at_k, :]
                above = jnp.where(row == OFF + BROW, u + CORNER_WEIGHT * beside(u), above)
        return r_all[p] + (below + above)

    for k, omega in enumerate(OMEGAS):
        f = None
        for p in range(BY):
            if k > 0:
                r = gathered(p, k)
                r_all[p] = r
            else:
                r = r_all[p]
            f = (r if f is None else r + f) * inverse[p]
            f_all[p] = f
        s = None
        for p in reversed(range(BY)):
            s = f_all[p] if s is None else f_all[p] + inverse[p] * s
            if k == 0:
                u = s * (1.0 / GAMMA)
            else:
                u = omega * s + (GAMMA * omega - 1.0) * u_all[k - 1, p]
            u_all[k, p] = u
            h = beside(u)
            t_all[p] = u + CORNER_WEIGHT * h
            r_all[p] = r_all[p] + (h - d_all[p] * u)
        if k == 1:
            for strip, p, n in ((south, 0, OFF - 1), (north, BY - 1, OFF + BROW)):
                s = strip[at + 2 : at + 3, :] + strip[at + 3 : at + 4, :] * t_all[p, n : n + 1, :]
                u = OMEGAS[2] * s + (GAMMA * OMEGAS[2] - 1.0) * strip[at + 1 : at + 2, :]
                strip[at + 2 : at + 3, :] = u
    for p in range(BY):
        r = jnp.where(d_all[p] > 1.0, gathered(p, ITERS), 0.0)
        start = x_wide[p]
        if p == 0:
            start = jnp.where(row == OFF + BROW, north[at + 5 : at + 6, :], start)
        x = start + ((u_all[0, p] + u_all[1, p]) + (u_all[2, p] + u_all[3, p]))
        f_all[p] = x
        for q in range(BCOL):
            cols = slice(BX * q, BX * q + BX)
            natural[q, pl.ds(p, BROW, stride=BY), :] = x[OFF : OFF + BROW, cols]
            natural[BCOL + q, pl.ds(p, BROW, stride=BY), :] = r[OFF : OFF + BROW, cols]
    copies = []
    for k, out in enumerate((solution, residual)):
        for q in range(BCOL):
            n = BCOL * k + q
            copies.append(pltpu.make_async_copy(natural.at[n], out.at[:, pl.ds(BX * q, BX)], sems.at[n]))
    for copy in copies:
        copy.start()
    for p in range(BY):
        x = f_all[p]
        ocean = d_all[p] > 1.0
        above = f_all[p + 1] if p + 1 < BY else pltpu.roll(f_all[0], EXT - 1, 0)
        zonal = jnp.where(ocean, pltpu.roll(x, WIDE - 1, 1) - x, 0.0)
        meridional = jnp.where(ocean, above - x, 0.0)
        for q in range(BCOL):
            cols = slice(BX * q, BX * q + BX)
            g_all[q, EXT * p : EXT * p + EXT, :] = zonal[:, cols]
            g_all[BCOL + q, EXT * p : EXT * p + EXT, :] = meridional[:, cols]

    def take(slot, carry):
        index = loc[slot]
        row, col = (index >> 2) + OFF, index & 3
        slots[slot, 0] = g_all[col, pl.ds(row, BY, stride=EXT), :]
        slots[slot, 1] = g_all[BCOL + col, pl.ds(row, BY, stride=EXT), :]
        return carry

    lax.fori_loop(0, slots.shape[0], take, 0, unroll=8)
    for copy in copies:
        copy.wait()


def pick_kernel(dst, slots, out, sems):
    copies = [
        pltpu.make_async_copy(slots.at[dst[n]], out.at[n], sems.at[n]) for n in range(out.shape[0])
    ]
    for copy in copies:
        copy.start()
    for copy in copies:
        copy.wait()


def body(tendencies, thickness, ocean_blocks, land_mask, implicit_term, first_guess):
    nx = lax.axis_size("gx")
    ny = lax.axis_size("gy")
    gx = lax.axis_index("gx")
    gy = lax.axis_index("gy")
    devices = nx * ny
    listed = tendencies.shape[0]
    me = gx * ny + gy
    block_cols = BCOL * nx
    block_row = ocean_blocks // block_cols
    block_col = ocean_blocks % block_cols
    owner = block_col // BCOL * ny + block_row // BROW
    local = block_row % BROW * BCOL + block_col % BCOL
    dst = lax.dynamic_slice_in_dim(owner, me * listed, listed)
    loc = jnp.min(jnp.where(owner == me, local, BROW * BCOL).reshape(devices, listed), axis=1)
    device = jnp.arange(devices, dtype=jnp.int32)
    came = [(loc[None, :] == jnp.arange(BROW * BCOL, dtype=jnp.int32)[:, None])]
    for step, at in ((1, 0), (nx - 1, BCOL - 1)):
        here = (owner == (gx + step) % nx * ny + gy) & (local % BCOL == at)
        side = jnp.min(jnp.where(here, local // BCOL, BROW).reshape(devices, listed), axis=1)
        came.append(side[None, :] == jnp.arange(BROW, dtype=jnp.int32)[:, None])
    came = jnp.max(jnp.where(jnp.concatenate(came), device[None, :], 0), axis=1)
    flags = jnp.stack([gy % 2, (gy == ny - 1).astype(jnp.int32)]).astype(jnp.int32)

    east = [(i, (i + 1) % nx) for i in range(nx)]
    west = [(j, i) for i, j in east]
    swap_a, swap_b = [], []
    for i in range(nx):
        for j in range(ny):
            swap_a.append((i * ny + j, i * ny + (j ^ 1)))
            if j == ny - 1:
                swap_b.append((i * ny + j, (nx - 1 - i) * ny + j))
            elif j > 0:
                swap_b.append((i * ny + j, i * ny + (j + 1 if j % 2 else j - 1)))

    def exchange_x(to_east, to_west):
        return lax.ppermute(to_west, "gx", west), lax.ppermute(to_east, "gx", east)

    hbm = pl.BlockSpec(memory_space=pltpu.HBM)
    back = (devices, 2, BY, BX)
    sums = pl.pallas_call(
        sums_kernel,
        out_shape=jax.ShapeDtypeStruct((devices, 2 * BY // 4 + 1, 4, BX), F32),
        in_specs=[pl.BlockSpec(memory_space=pltpu.SMEM), hbm, hbm],
        out_specs=hbm,
        scratch_shapes=[
            pltpu.VMEM(tendencies.shape, tendencies.dtype),
            pltpu.SMEM(ocean_blocks.shape, jnp.int32),
            pltpu.VMEM((listed, 2 * BY // 4, 4, BX), F32),
            pltpu.VMEM((devices + 1, 4, BX), F32),
            pltpu.VMEM((LEV, BY, BX), F32),
            pltpu.SemaphoreType.DMA((listed // CHUNK,)),
            pltpu.SemaphoreType.DMA((listed,)),
            pltpu.SemaphoreType.DMA((2,)),
        ],
        compiler_params=pltpu.CompilerParams(vmem_limit_bytes=58 * MIB),
    )(thickness, ocean_blocks, tendencies)
    arrived = lax.all_to_all(sums, ("gx", "gy"), split_axis=0, concat_axis=0, tiled=True)

    own = (BY, EXT, BCOL * BX)
    tile = (BROW * BY, BCOL * BX)
    full = (BY, EXT, WIDE)
    strip = (STRIP, WIDE)
    sent = (SENT, BCOL * BX)
    sums, land_mask, implicit_term, first_guess = lax.optimization_barrier(
        (sums, land_mask, implicit_term, first_guess)
    )
    fields, to_east, to_west = call(
        prepare_kernel,
        [(2, *own), (2 * EXT, BX), (2 * EXT, BX)],
        [land_mask, implicit_term, first_guess],
        [(2 * BCOL, BROW * BY, BX)],
        58,
    )
    from_sides = exchange_x(to_east, to_west)

    small = (BY, 16, WIDE)
    first, second = call(
        ends_kernel,
        [sent, sent],
        [flags, came, arrived, fields, *from_sides],
        [(2 * (BCOL + 2), BY * 16, BX), small, small, small, small, small, small, strip, strip, strip],
        12,
    )
    came, first, second = lax.optimization_barrier((came, first, second))
    first = lax.ppermute(first, ("gx", "gy"), swap_a)
    second = lax.ppermute(second, ("gx", "gy"), swap_b)
    r_wide, d_wide, x_wide, inverse, edges = call(
        right_kernel,
        [full, full, full, full, (8, WIDE)],
        [came, arrived, fields, *from_sides],
        [(2 * (BCOL + 2), BY * EXT, BX), full],
        12,
    )
    vmem = pl.BlockSpec(memory_space=pltpu.VMEM)
    smem = pl.BlockSpec(memory_space=pltpu.SMEM)
    solution, residual, slots = pl.pallas_call(
        solve_kernel,
        out_shape=[jax.ShapeDtypeStruct(a, F32) for a in (tile, tile, back)],
        in_specs=[smem, smem] + [vmem] * 7,
        out_specs=[hbm, hbm, vmem],
        scratch_shapes=[pltpu.VMEM(full, F32)] * 5
        + [
            pltpu.VMEM((ITERS, *full), F32),
            pltpu.VMEM((2 * BCOL, BY * EXT, BX), F32),
            pltpu.VMEM((2 * BCOL, BROW * BY, BX), F32),
            pltpu.VMEM(strip, F32),
            pltpu.VMEM(strip, F32),
            pltpu.SemaphoreType.DMA((2 * BCOL,)),
        ],
        compiler_params=pltpu.CompilerParams(vmem_limit_bytes=18 * MIB),
    )(flags, loc, r_wide, d_wide, x_wide, inverse, edges, first, second)
    returned = lax.all_to_all(slots, ("gx", "gy"), split_axis=0, concat_axis=0, tiled=True)
    gradient_blocks = pl.pallas_call(
        pick_kernel,
        out_shape=jax.ShapeDtypeStruct((listed, 2, BY, BX), F32),
        in_specs=[pl.BlockSpec(memory_space=pltpu.SMEM), pl.BlockSpec(memory_space=pltpu.VMEM)],
        out_specs=pl.BlockSpec(memory_space=pl.ANY),
        scratch_shapes=[pltpu.SemaphoreType.DMA((listed,))],
        compiler_params=pltpu.CompilerParams(vmem_limit_bytes=4 * MIB),
    )(dst, returned)
    return solution, residual, gradient_blocks


def solution(mesh):
    placed = (
        P(("gx", "gy"), None, None, None, None),
        P(),
        P(),
        P("gy", "gx"),
        P("gy", "gx"),
        P("gy", "gx"),
    )
    return jax.shard_map(
        body,
        mesh=mesh,
        in_specs=placed,
        out_specs=(P("gy", "gx"), P("gy", "gx"), P(("gx", "gy"), None, None, None)),
        check_vma=False,
    )
```

```python
import functools

import jax
import jax.numpy as jnp
from jax import lax
from jax.experimental import pallas as pl
from jax.experimental.pallas import tpu as pltpu
from jax.sharding import PartitionSpec as P

BX = 128
BY = 16
BCOL = 4
BROW = 20
LEV = 24
ITERS = 4
STENCIL_SUM = 5.0
CORNER_WEIGHT = 0.25
LOWER_BOUND = 0.02
UPPER_BOUND = 2.0

F32 = jnp.float32
EXT = BROW + 4
OFF = 2
DEPTH = 1
WIDE = BCOL * BX + BX
PART = DEPTH * BY
SINGLE = 6
STRIP = 2 * PART + 8
SENT = STRIP
CHUNK = 4
MIB = 1 << 20
GAMMA = (UPPER_BOUND + LOWER_BOUND) / 2.0
SCALE = 4.0 * (2.0 / (UPPER_BOUND - LOWER_BOUND)) ** 2
OMEGAS = [2.0 / GAMMA]
for _ in range(1, ITERS):
    OMEGAS.append(1.0 / (GAMMA - OMEGAS[-1] / SCALE))


def call(kernel, out_shape, operands, scratch, vmem):
    spaces = [
        pl.BlockSpec(memory_space=pltpu.SMEM if a.dtype == jnp.int32 and a.ndim == 1 else pltpu.VMEM)
        for a in operands
    ]
    return pl.pallas_call(
        kernel,
        out_shape=[jax.ShapeDtypeStruct(s, F32) for s in out_shape],
        in_specs=spaces,
        out_specs=[pl.BlockSpec(memory_space=pltpu.VMEM) for _ in out_shape],
        scratch_shapes=[pltpu.VMEM(s, F32) for s in scratch],
        compiler_params=pltpu.CompilerParams(vmem_limit_bytes=vmem * MIB),
        cost_estimate=pl.CostEstimate(flops=1, bytes_accessed=1, transcendentals=0),
    )(*operands)


def lanes(shape):
    return lax.broadcasted_iota(jnp.int32, shape, 1)


def rows(shape):
    return lax.broadcasted_iota(jnp.int32, shape, 0)


def pack(tiles, last):
    lane = lanes(tiles[0].shape)
    packed = jnp.zeros(tiles[0].shape, F32)
    for p, tile in enumerate(tiles):
        shift = (8 * p + 8 if last else 8 * p) % BX
        moved = pltpu.roll(tile, shift, 1) if shift else tile
        packed = jnp.where(lane // 8 == p, moved, packed)
    return packed


def unpack(packed, p, at):
    shift = (at - 8 * p) % BX
    return pltpu.roll(packed, shift, 1) if shift else packed


def side_tile(east, west, p):
    lane = lanes(east.shape)
    tile = jnp.where(lane < 8, unpack(east, p, 0), 0.0)
    return jnp.where(lane >= BX - 8, unpack(west, p, BX - 8), tile)


def turned(strip):
    lane = BX - 1 - lanes((strip.shape[0], BX))
    tiles = [strip[:, BX * q : BX * q + BX] for q in range(WIDE // BX)]
    tiles = [jnp.take_along_axis(tile, lane, axis=1) for tile in tiles]
    return jnp.concatenate([tiles[(BCOL - 1 - q) % (BCOL + 1)] for q in range(BCOL + 1)], axis=1)


def beside(value):
    return pltpu.roll(value, 1, 1) + pltpu.roll(value, WIDE - 1, 1)


def send(strip, message):
    message[0 : 2 * PART, :] = strip[0 : 2 * PART, 0 : BCOL * BX]
    lane = lanes((8, BX))
    packed = jnp.zeros((8, BX), F32)
    for g in range(STRIP // 8):
        tile = strip[8 * g : 8 * g + 8, BCOL * BX : WIDE]
        packed = jnp.where(lane // 16 == g, pltpu.roll(tile, (8 + 16 * g) % BX, 1), packed)
    message[2 * PART : SENT, 0:BX] = packed
    for k in range(SINGLE):
        for q in range(BCOL):
            n = BCOL * k + q
            cols = slice(BX * (1 + n // 8), BX * (2 + n // 8))
            message[2 * PART + n % 8 : 2 * PART + n % 8 + 1, cols] = strip[
                2 * PART + k : 2 * PART + k + 1, BX * q : BX * q + BX
            ]


def receive(message, strip):
    strip[0 : 2 * PART, 0 : BCOL * BX] = message[0 : 2 * PART, :]
    lane = lanes((8, BX))
    inside = (lane < 8) | (lane >= BX - 8)
    packed = message[2 * PART : SENT, 0:BX]
    for g in range(STRIP // 8):
        moved = pltpu.roll(packed, (BX - 8 - 16 * g) % BX, 1)
        strip[8 * g : 8 * g + 8, BCOL * BX : WIDE] = jnp.where(inside, moved, 0.0)
    for k in range(SINGLE):
        for q in range(BCOL):
            n = BCOL * k + q
            cols = slice(BX * (1 + n // 8), BX * (2 + n // 8))
            strip[2 * PART + k : 2 * PART + k + 1, BX * q : BX * q + BX] = message[
                2 * PART + n % 8 : 2 * PART + n % 8 + 1, cols
            ]


def sums_kernel(
    thickness, blocks, tendencies, out, buffer, listed, staged, edges, weights, sems, out_sems, other_sems
):
    count = buffer.shape[0]
    nx, ny = lax.axis_size("gx"), lax.axis_size("gy")
    me = lax.axis_index("gx") * ny + lax.axis_index("gy")
    listing = pltpu.make_async_copy(blocks, listed, other_sems.at[0])
    listing.start()

    def fetch(c):
        part = pl.ds(c * CHUNK, CHUNK)
        return pltpu.make_async_copy(tendencies.at[part], buffer.at[part], sems.at[c])

    def leave(n, owner):
        return pltpu.make_async_copy(staged.at[n], out.at[owner, pl.ds(0, 2 * BY // 4)], out_sems.at[n])

    row16, lane16 = rows((BY, BX)), lanes((BY, BX))
    row4 = rows((4, BX))

    for c in range(count // CHUNK):
        fetch(c).start()
    for level in range(LEV):
        weights[level] = jnp.full((BY, BX), thickness[level], F32)
    listing.wait()

    def chunk(c, carry):
        fetch(c).wait()
        for pair in range(CHUNK // 2):
            totals = [None] * 4
            for level in range(LEV):
                weight = weights[level]
                for k in range(4):
                    n = c * CHUNK + 2 * pair + k // 2
                    term = weight * buffer[n, k % 2, level].astype(F32)
                    totals[k] = term if totals[k] is None else totals[k] + term
            for k in range(2):
                n = c * CHUNK + 2 * pair + k
                index = listed[me * count + n]
                row, col = lax.div(index, BCOL * nx), lax.rem(index, BCOL * nx)
                tile_row, tile_col, at = lax.div(row, BROW), lax.div(col, BCOL), lax.rem(col, BCOL)
                both = totals[2 * k : 2 * k + 2]
                for part in range(2):
                    staged[n, 4 * part : 4 * part + 4] = both[part].reshape(4, 4, BX)
                leave(n, tile_col * ny + tile_row).start()
                east_edge = at == BCOL - 1
                source = lane16 % 8 + jnp.where(east_edge, BX - 8, 0)
                line = []
                for value in both:
                    spread = jnp.take_along_axis(value, source, axis=1)
                    spread = jnp.where(lane16 // 8 == row16, spread, 0.0)
                    line.append(jnp.sum(spread, axis=0, keepdims=True))
                beside_col = lax.rem(tile_col + jnp.where(east_edge, 1, nx - 1), nx)
                slot = jnp.where((at == 0) | east_edge, beside_col * ny + tile_row, edges.shape[0] - 1)
                value = jnp.where(row4 % 2 == 0, line[0], line[1])
                edges[slot] = jnp.where(row4 // 2 == jnp.where(east_edge, 1, 0), value, edges[slot])
        return carry

    lax.fori_loop(0, count // CHUNK, chunk, 0)
    sides = pltpu.make_async_copy(edges.at[pl.ds(0, nx * ny)], out.at[:, 2 * BY // 4], other_sems.at[1])
    sides.start()

    def finish(n, carry):
        leave(n, 0).wait()
        return carry

    lax.fori_loop(0, count, finish, 0)
    sides.wait()


def prepare_kernel(mask, implicit, guess, fields, to_east, to_west, work):
    for q in range(BCOL):
        cols = slice(BX * q, BX * q + BX)
        m = mask[:, cols].astype(F32)
        work[q] = m * (STENCIL_SUM + implicit[:, cols]) + (1.0 - m)
        work[BCOL + q] = m * guess[:, cols]
    edge = jnp.zeros((OFF, BX), F32)
    for k in range(2):
        for p in range(BY):
            for q in range(BCOL):
                tile = work[BCOL * k + q, pl.ds(p, BROW, stride=BY), :]
                tile = jnp.concatenate([edge, tile, edge], axis=0)
                fields[k, p, :, BX * q : BX * q + BX] = tile
        part = slice(EXT * k, EXT * k + EXT)
        to_west[part, :] = pack([fields[k, p, :, 0:BX] for p in range(BY)], False)
        to_east[part, :] = pack([fields[k, p, :, BX * (BCOL - 1) :] for p in range(BY)], True)


def put_blocks(came, arrived, work, first_row, count, height, offset):
    row16, lane16 = rows((BY, BX)), lanes((BY, BX))
    spread = 8 * row16 + lane16 % 8

    def put(n, carry):
        block_row = jnp.clip(first_row + n, 0, BROW - 1)
        at_rows = pl.ds(n + offset, BY, stride=height)
        for col in range(BCOL):
            slot = came[block_row * BCOL + col]
            for part in range(2):
                value = arrived[slot, 4 * part : 4 * part + 4].reshape(BY, BX)
                work[(BCOL + 2) * part + col, at_rows, :] = value
        for side in range(2):
            slot = came[(BCOL + side) * BROW + block_row]
            for part in range(2):
                line = arrived[slot, 8, 2 * side + part : 2 * side + part + 1]
                value = jnp.take_along_axis(jnp.broadcast_to(line, (BY, BX)), spread, axis=1)
                work[(BCOL + 2) * part + BCOL + side, at_rows, :] = value
        return carry

    lax.fori_loop(0, count, put, 0, unroll=min(count, 10))


def right_side(work, fields, east, west, parts, r_wide, d_wide, x_wide, inverse, tall):
    height = sum(high - low for low, high in parts)
    for k, wide in enumerate((d_wide, x_wide)):
        sides = [
            jnp.concatenate([side[EXT * k + low : EXT * k + high, :] for low, high in parts], axis=0)
            for side in (east, west)
        ]
        for p in range(BY):
            at = 0
            for low, high in parts:
                wide[p, at : at + high - low, 0 : BCOL * BX] = fields[k, p, low:high, :]
                at += high - low
            wide[p, :, BCOL * BX : WIDE] = side_tile(*sides, p)
    previous = None
    for p in range(BY):
        d = d_wide[p]
        previous = jnp.where(d > 1.0, 1.0 / (d if p == 0 else d - previous), 0.0)
        inverse[p] = previous
        x = x_wide[p]
        tall[p] = x + CORNER_WEIGHT * beside(x)
    lane = lanes((height, BX))

    def forcing(part, p):
        at = slice(height * p, height * p + height)
        tiles = [work[(BCOL + 2) * part + q, at, :] for q in range(BCOL + 2)]
        tiles[BCOL] = jnp.where(lane < BX // 2, tiles[BCOL], tiles[BCOL + 1])
        value = jnp.concatenate(tiles[: BCOL + 1], axis=1)
        return jnp.where(d_wide[p] > 1.0, value, 0.0)

    last = forcing(1, BY - 1)
    south = pltpu.roll(last, 1, 0)
    for p in range(BY):
        f0 = forcing(0, p)
        f1 = forcing(1, p) if p + 1 < BY else last
        below = tall[p - 1] if p > 0 else pltpu.roll(tall[BY - 1], 1, 0)
        above = tall[p + 1] if p + 1 < BY else pltpu.roll(tall[0], height - 1, 0)
        x = x_wide[p]
        minus_a = beside(x) + (below + above) - d_wide[p] * x
        r_wide[p] = (f0 - pltpu.roll(f0, 1, 1)) + (f1 - south) + minus_a
        south = f1
    return last


def right_kernel(
    came, arrived, fields, east, west,
    r_wide, d_wide, x_wide, inverse, edges,
    work, tall,
):
    put_blocks(came, arrived, work, 0, BROW, EXT, OFF)
    last = right_side(work, fields, east, west, ((0, EXT),), r_wide, d_wide, x_wide, inverse, tall)
    t_top = tall[BY - 1, OFF + BROW - 1 : OFF + BROW, :]
    edges[0:1, :] = t_top - last[OFF + BROW - 1 : OFF + BROW, :]
    edges[1:2, :] = t_top
    edges[2:3, :] = tall[0, OFF : OFF + 1, :]
    edges[3:8, :] = jnp.zeros((5, WIDE), F32)


def ends_kernel(
    flags, came, arrived, fields, east, west, first, second,
    work, r_wide, d_wide, x_wide, inverse, tall, update, top, bottom, flipped,
):
    put_blocks(came, arrived, work, -OFF, 8, 16, 0)
    put_blocks(came, arrived, work, EXT - 8 - OFF, 8, 16, 8)
    parts = ((0, 8), (EXT - 8, EXT))
    last = right_side(work, fields, east, west, parts, r_wide, d_wide, x_wide, inverse, tall)
    at = 2 * PART
    south, north = OFF, 16 - OFF - 1
    for k, wide in enumerate((r_wide, d_wide)):
        for p in range(BY):
            part = slice(PART * k + DEPTH * p, PART * k + DEPTH * p + DEPTH)
            top[part, :] = wide[p, north : north + DEPTH, :]
            bottom[part, :] = wide[p, south : south + DEPTH, :]
    t_top = tall[BY - 1, north : north + 1, :]
    top[at + 4 : at + 5, :] = t_top - jnp.where(flags[1] == 1, 0.0, last[north : north + 1, :])
    top[at + 5 : at + 6, :] = x_wide[BY - 1, north : north + 1, :]
    bottom[at + 4 : at + 5, :] = tall[0, south : south + 1, :]
    bottom[at + 5 : at + 6, :] = x_wide[0, south : south + 1, :]

    def line():
        lower = []
        for p in range(BY):
            r = r_wide[p] if p == 0 else r_wide[p] + lower[-1]
            lower.append(r * inverse[p])
        upper = [lower[-1]]
        for p in range(BY - 2, -1, -1):
            upper.append(lower[p] + inverse[p] * upper[-1])
        return upper[::-1]

    behind = ((0, south + 1, bottom), (BY - 1, north - 1, top))
    row = rows((16, WIDE))
    strips = (row == south) | (row == north)
    for k in range(2):
        for p, s in enumerate(line()):
            u = s * (1.0 / GAMMA) if k == 0 else OMEGAS[1] * s + (GAMMA * OMEGAS[1] - 1.0) * update[p]
            update[p] = u
            t = u + CORNER_WEIGHT * beside(u)
            tall[p] = t if k == 0 else jnp.where(strips, 0.0, t)
        for p in range(BY):
            below = tall[p - 1] if p > 0 else pltpu.roll(tall[BY - 1], 1, 0)
            above = tall[p + 1] if p + 1 < BY else pltpu.roll(tall[0], 15, 0)
            u = update[p]
            r_wide[p] = r_wide[p] + (beside(u) + (below + above) - d_wide[p] * u)
        for p, n, strip in behind:
            strip[at + k : at + k + 1, :] = update[p, n : n + 1, :]
    smoothed = line()
    element = None
    for p in reversed(range(BY)):
        d = d_wide[p]
        element = jnp.where(d > 1.0, 1.0 / (d if element is None else d - element), 0.0)
    for (p, n, strip), diagonal in zip(behind, (element, inverse[BY - 1])):
        strip[at + 2 : at + 3, :] = smoothed[p][n : n + 1, :]
        strip[at + 3 : at + 4, :] = diagonal[n : n + 1, :]
        strip[at + SINGLE : STRIP, :] = jnp.zeros((STRIP - at - SINGLE, WIDE), F32)

    @pl.when(flags[1] == 1)
    def _():
        for k in range(2):
            for r in range(PART):
                flipped[PART * k + r : PART * k + r + 1, :] = top[PART * (k + 1) - 1 - r : PART * (k + 1) - r, :]
        flipped[at:STRIP, :] = top[at:STRIP, :]
        top[...] = turned(flipped[...])

    @pl.when(flags[0] == 1)
    def _():
        send(bottom, first)
        send(top, second)

    @pl.when(flags[0] == 0)
    def _():
        send(top, first)
        send(bottom, second)


def solve_kernel(
    flags, loc, r_wide, d_wide, x_wide, inverse_own, edges, first, second,
    solution, residual, slots,
    r_all, d_all, inverse, f_all, t_all, u_all, g_all, natural, south, north, sems,
):
    @pl.when(flags[0] == 1)
    def _():
        receive(first, south)
        receive(second, north)

    @pl.when(flags[0] == 0)
    def _():
        receive(second, south)
        receive(first, north)

    row = rows((EXT, WIDE))
    for k, (field, out) in enumerate(((r_wide, r_all), (d_wide, d_all))):
        for p in range(BY):
            part = slice(PART * k + DEPTH * p, PART * k + DEPTH * p + DEPTH)
            out[p] = field[p]
            out[p, OFF - DEPTH : OFF, :] = south[part, :]
            out[p, OFF + BROW : OFF + BROW + DEPTH, :] = north[part, :]
    previous = None
    for p in range(BY):
        d = jnp.concatenate([d_all[p, 0:8, :], d_all[p, EXT - 8 : EXT, :]], axis=0)
        previous = jnp.where(d > 1.0, 1.0 / (d if p == 0 else d - previous), 0.0)
        inverse[p, 0:8, :] = previous[0:8, :]
        inverse[p, 8 : EXT - 8, :] = inverse_own[p, 8 : EXT - 8, :]
        inverse[p, EXT - 8 : EXT, :] = previous[8:16, :]
    at = 2 * PART
    upward = jnp.where(flags[1] == 1, edges[1:2, :], edges[0:1, :])
    fix = jnp.where(row == OFF, south[at + 4 : at + 5, :], 0.0)
    r_all[0] = r_all[0] + jnp.where(row == OFF + BROW, upward, fix)
    fix = jnp.where(row == OFF + BROW - 1, north[at + 4 : at + 5, :], 0.0)
    r_all[BY - 1] = r_all[BY - 1] + jnp.where(row == OFF - 1, edges[2:3, :], fix)

    def gathered(p, k):
        below = t_all[p - 1] if p > 0 else pltpu.roll(t_all[BY - 1], 1, 0)
        above = t_all[p + 1] if p + 1 < BY else pltpu.roll(t_all[0], EXT - 1, 0)
        if k < ITERS:
            at_k = slice(at + k - 1, at + k)
            if p == 0:
                u = south[at_k, :]
                below = jnp.where(row == OFF - 1, u + CORNER_WEIGHT * beside(u), below)
            if p == BY - 1:
                u = north[at_k, :]
                above = jnp.where(row == OFF + BROW, u + CORNER_WEIGHT * beside(u), above)
        return r_all[p] + (below + above)

    for k, omega in enumerate(OMEGAS):
        f = None
        for p in range(BY):
            if k > 0:
                r = gathered(p, k)
                r_all[p] = r
            else:
                r = r_all[p]
            f = (r if f is None else r + f) * inverse[p]
            f_all[p] = f
        s = None
        for p in reversed(range(BY)):
            s = f_all[p] if s is None else f_all[p] + inverse[p] * s
            if k == 0:
                u = s * (1.0 / GAMMA)
            else:
                u = omega * s + (GAMMA * omega - 1.0) * u_all[k - 1, p]
            u_all[k, p] = u
            h = beside(u)
            t_all[p] = u + CORNER_WEIGHT * h
            r_all[p] = r_all[p] + (h - d_all[p] * u)
        if k == 1:
            for strip, p, n in ((south, 0, OFF - 1), (north, BY - 1, OFF + BROW)):
                s = strip[at + 2 : at + 3, :] + strip[at + 3 : at + 4, :] * t_all[p, n : n + 1, :]
                u = OMEGAS[2] * s + (GAMMA * OMEGAS[2] - 1.0) * strip[at + 1 : at + 2, :]
                strip[at + 2 : at + 3, :] = u
    for p in range(BY):
        r = jnp.where(d_all[p] > 1.0, gathered(p, ITERS), 0.0)
        start = x_wide[p]
        if p == 0:
            start = jnp.where(row == OFF + BROW, north[at + 5 : at + 6, :], start)
        x = start + ((u_all[0, p] + u_all[1, p]) + (u_all[2, p] + u_all[3, p]))
        f_all[p] = x
        for q in range(BCOL):
            cols = slice(BX * q, BX * q + BX)
            natural[q, pl.ds(p, BROW, stride=BY), :] = x[OFF : OFF + BROW, cols]
            natural[BCOL + q, pl.ds(p, BROW, stride=BY), :] = r[OFF : OFF + BROW, cols]
    copies = []
    for k, out in enumerate((solution, residual)):
        for q in range(BCOL):
            n = BCOL * k + q
            copies.append(pltpu.make_async_copy(natural.at[n], out.at[:, pl.ds(BX * q, BX)], sems.at[n]))
    for copy in copies:
        copy.start()
    for p in range(BY):
        x = f_all[p]
        ocean = d_all[p] > 1.0
        above = f_all[p + 1] if p + 1 < BY else pltpu.roll(f_all[0], EXT - 1, 0)
        zonal = jnp.where(ocean, pltpu.roll(x, WIDE - 1, 1) - x, 0.0)
        meridional = jnp.where(ocean, above - x, 0.0)
        for q in range(BCOL):
            cols = slice(BX * q, BX * q + BX)
            g_all[q, EXT * p : EXT * p + EXT, :] = zonal[:, cols]
            g_all[BCOL + q, EXT * p : EXT * p + EXT, :] = meridional[:, cols]

    def take(slot, carry):
        index = loc[slot]
        row, col = (index >> 2) + OFF, index & 3
        slots[slot, 0] = g_all[col, pl.ds(row, BY, stride=EXT), :]
        slots[slot, 1] = g_all[BCOL + col, pl.ds(row, BY, stride=EXT), :]
        return carry

    lax.fori_loop(0, slots.shape[0], take, 0, unroll=16)
    for copy in copies:
        copy.wait()


def pick_kernel(dst, slots, out, picked, sems):
    part = picked.shape[0] // sems.shape[0]
    copies = []
    for c in range(sems.shape[0]):
        for n in range(part * c, part * c + part):
            picked[n] = slots[dst[n]]
        at = pl.ds(part * c, part)
        copies.append(pltpu.make_async_copy(picked.at[at], out.at[at], sems.at[c]))
        copies[-1].start()
    for copy in copies:
        copy.wait()


def body(tendencies, thickness, ocean_blocks, land_mask, implicit_term, first_guess):
    nx = lax.axis_size("gx")
    ny = lax.axis_size("gy")
    gx = lax.axis_index("gx")
    gy = lax.axis_index("gy")
    devices = nx * ny
    listed = tendencies.shape[0]
    me = gx * ny + gy
    block_cols = BCOL * nx
    block_row = ocean_blocks // block_cols
    block_col = ocean_blocks % block_cols
    owner = block_col // BCOL * ny + block_row // BROW
    local = block_row % BROW * BCOL + block_col % BCOL
    dst = lax.dynamic_slice_in_dim(owner, me * listed, listed)
    loc = jnp.min(jnp.where(owner == me, local, BROW * BCOL).reshape(devices, listed), axis=1)
    device = jnp.arange(devices, dtype=jnp.int32)
    came = [(loc[None, :] == jnp.arange(BROW * BCOL, dtype=jnp.int32)[:, None])]
    for step, at in ((1, 0), (nx - 1, BCOL - 1)):
        here = (owner == (gx + step) % nx * ny + gy) & (local % BCOL == at)
        side = jnp.min(jnp.where(here, local // BCOL, BROW).reshape(devices, listed), axis=1)
        came.append(side[None, :] == jnp.arange(BROW, dtype=jnp.int32)[:, None])
    came = jnp.max(jnp.where(jnp.concatenate(came), device[None, :], 0), axis=1)
    flags = jnp.stack([gy % 2, (gy == ny - 1).astype(jnp.int32)]).astype(jnp.int32)

    east = [(i, (i + 1) % nx) for i in range(nx)]
    west = [(j, i) for i, j in east]
    swap_a, swap_b = [], []
    for i in range(nx):
        for j in range(ny):
            swap_a.append((i * ny + j, i * ny + (j ^ 1)))
            if j == ny - 1:
                swap_b.append((i * ny + j, (nx - 1 - i) * ny + j))
            elif j > 0:
                swap_b.append((i * ny + j, i * ny + (j + 1 if j % 2 else j - 1)))

    def exchange_x(to_east, to_west):
        return lax.ppermute(to_west, "gx", west), lax.ppermute(to_east, "gx", east)

    hbm = pl.BlockSpec(memory_space=pltpu.HBM)
    back = (devices, 2, BY, BX)
    sums = pl.pallas_call(
        sums_kernel,
        out_shape=jax.ShapeDtypeStruct((devices, 2 * BY // 4 + 1, 4, BX), F32),
        in_specs=[pl.BlockSpec(memory_space=pltpu.SMEM), hbm, hbm],
        out_specs=hbm,
        scratch_shapes=[
            pltpu.VMEM(tendencies.shape, tendencies.dtype),
            pltpu.SMEM(ocean_blocks.shape, jnp.int32),
            pltpu.VMEM((listed, 2 * BY // 4, 4, BX), F32),
            pltpu.VMEM((devices + 1, 4, BX), F32),
            pltpu.VMEM((LEV, BY, BX), F32),
            pltpu.SemaphoreType.DMA((listed // CHUNK,)),
            pltpu.SemaphoreType.DMA((listed,)),
            pltpu.SemaphoreType.DMA((2,)),
        ],
        compiler_params=pltpu.CompilerParams(vmem_limit_bytes=58 * MIB),
    )(thickness, ocean_blocks, tendencies)
    arrived = lax.all_to_all(sums, ("gx", "gy"), split_axis=0, concat_axis=0, tiled=True)

    own = (BY, EXT, BCOL * BX)
    tile = (BROW * BY, BCOL * BX)
    full = (BY, EXT, WIDE)
    strip = (STRIP, WIDE)
    sent = (SENT, BCOL * BX)
    sums, land_mask, implicit_term, first_guess = lax.optimization_barrier(
        (sums, land_mask, implicit_term, first_guess)
    )
    fields, to_east, to_west = call(
        prepare_kernel,
        [(2, *own), (2 * EXT, BX), (2 * EXT, BX)],
        [land_mask, implicit_term, first_guess],
        [(2 * BCOL, BROW * BY, BX)],
        58,
    )
    from_sides = exchange_x(to_east, to_west)

    small = (BY, 16, WIDE)
    first, second = call(
        ends_kernel,
        [sent, sent],
        [flags, came, arrived, fields, *from_sides],
        [(2 * (BCOL + 2), BY * 16, BX), small, small, small, small, small, small, strip, strip, strip],
        12,
    )
    came, first, second = lax.optimization_barrier((came, first, second))
    first = lax.ppermute(first, ("gx", "gy"), swap_a)
    second = lax.ppermute(second, ("gx", "gy"), swap_b)
    r_wide, d_wide, x_wide, inverse, edges = call(
        right_kernel,
        [full, full, full, full, (8, WIDE)],
        [came, arrived, fields, *from_sides],
        [(2 * (BCOL + 2), BY * EXT, BX), full],
        12,
    )
    vmem = pl.BlockSpec(memory_space=pltpu.VMEM)
    smem = pl.BlockSpec(memory_space=pltpu.SMEM)
    solution, residual, slots = pl.pallas_call(
        solve_kernel,
        out_shape=[jax.ShapeDtypeStruct(a, F32) for a in (tile, tile, back)],
        in_specs=[smem, smem] + [vmem] * 7,
        out_specs=[hbm, hbm, vmem],
        scratch_shapes=[pltpu.VMEM(full, F32)] * 5
        + [
            pltpu.VMEM((ITERS, *full), F32),
            pltpu.VMEM((2 * BCOL, BY * EXT, BX), F32),
            pltpu.VMEM((2 * BCOL, BROW * BY, BX), F32),
            pltpu.VMEM(strip, F32),
            pltpu.VMEM(strip, F32),
            pltpu.SemaphoreType.DMA((2 * BCOL,)),
        ],
        compiler_params=pltpu.CompilerParams(vmem_limit_bytes=18 * MIB),
    )(flags, loc, r_wide, d_wide, x_wide, inverse, edges, first, second)
    returned = lax.all_to_all(slots, ("gx", "gy"), split_axis=0, concat_axis=0, tiled=True)
    gradient_blocks = pl.pallas_call(
        pick_kernel,
        out_shape=jax.ShapeDtypeStruct((listed, 2, BY, BX), F32),
        in_specs=[pl.BlockSpec(memory_space=pltpu.SMEM), pl.BlockSpec(memory_space=pltpu.VMEM)],
        out_specs=pl.BlockSpec(memory_space=pl.ANY),
        scratch_shapes=[pltpu.VMEM((listed, 2, BY, BX), F32), pltpu.SemaphoreType.DMA((4,))],
        compiler_params=pltpu.CompilerParams(vmem_limit_bytes=4 * MIB),
    )(dst, returned)
    return solution, residual, gradient_blocks


def solution(mesh):
    placed = (
        P(("gx", "gy"), None, None, None, None),
        P(),
        P(),
        P("gy", "gx"),
        P("gy", "gx"),
        P("gy", "gx"),
    )
    return jax.shard_map(
        body,
        mesh=mesh,
        in_specs=placed,
        out_specs=(P("gy", "gx"), P("gy", "gx"), P(("gx", "gy"), None, None, None)),
        check_vma=False,
    )
```

```python
import functools

import jax
import jax.numpy as jnp
from jax import lax
from jax.experimental import pallas as pl
from jax.experimental.pallas import tpu as pltpu
from jax.sharding import PartitionSpec as P

BX = 128
BY = 16
BCOL = 4
BROW = 20
LEV = 24
ITERS = 4
STENCIL_SUM = 5.0
CORNER_WEIGHT = 0.25
LOWER_BOUND = 0.02
UPPER_BOUND = 2.0

F32 = jnp.float32
EXT = BROW + 4
OFF = 2
DEPTH = 1
WIDE = BCOL * BX + BX
PART = DEPTH * BY
SINGLE = 6
STRIP = 2 * PART + 8
SENT = STRIP
CHUNK = 4
MIB = 1 << 20
GAMMA = (UPPER_BOUND + LOWER_BOUND) / 2.0
SCALE = 4.0 * (2.0 / (UPPER_BOUND - LOWER_BOUND)) ** 2
OMEGAS = [2.0 / GAMMA]
for _ in range(1, ITERS):
    OMEGAS.append(1.0 / (GAMMA - OMEGAS[-1] / SCALE))


def call(kernel, out_shape, operands, scratch, vmem):
    spaces = [
        pl.BlockSpec(memory_space=pltpu.SMEM if a.dtype == jnp.int32 and a.ndim == 1 else pltpu.VMEM)
        for a in operands
    ]
    return pl.pallas_call(
        kernel,
        out_shape=[jax.ShapeDtypeStruct(s, F32) for s in out_shape],
        in_specs=spaces,
        out_specs=[pl.BlockSpec(memory_space=pltpu.VMEM) for _ in out_shape],
        scratch_shapes=[pltpu.VMEM(s, F32) for s in scratch],
        compiler_params=pltpu.CompilerParams(vmem_limit_bytes=vmem * MIB),
        cost_estimate=pl.CostEstimate(flops=1, bytes_accessed=1, transcendentals=0),
    )(*operands)


def lanes(shape):
    return lax.broadcasted_iota(jnp.int32, shape, 1)


def rows(shape):
    return lax.broadcasted_iota(jnp.int32, shape, 0)


def pack(tiles, last):
    lane = lanes(tiles[0].shape)
    packed = jnp.zeros(tiles[0].shape, F32)
    for p, tile in enumerate(tiles):
        shift = (8 * p + 8 if last else 8 * p) % BX
        moved = pltpu.roll(tile, shift, 1) if shift else tile
        packed = jnp.where(lane // 8 == p, moved, packed)
    return packed


def unpack(packed, p, at):
    shift = (at - 8 * p) % BX
    return pltpu.roll(packed, shift, 1) if shift else packed


def side_tile(east, west, p):
    lane = lanes(east.shape)
    tile = jnp.where(lane < 8, unpack(east, p, 0), 0.0)
    return jnp.where(lane >= BX - 8, unpack(west, p, BX - 8), tile)


def turned(strip):
    lane = BX - 1 - lanes((strip.shape[0], BX))
    tiles = [strip[:, BX * q : BX * q + BX] for q in range(WIDE // BX)]
    tiles = [jnp.take_along_axis(tile, lane, axis=1) for tile in tiles]
    return jnp.concatenate([tiles[(BCOL - 1 - q) % (BCOL + 1)] for q in range(BCOL + 1)], axis=1)


def beside(value):
    return pltpu.roll(value, 1, 1) + pltpu.roll(value, WIDE - 1, 1)


def send(strip, message):
    message[0 : 2 * PART, :] = strip[0 : 2 * PART, 0 : BCOL * BX]
    lane = lanes((8, BX))
    packed = jnp.zeros((8, BX), F32)
    for g in range(STRIP // 8):
        tile = strip[8 * g : 8 * g + 8, BCOL * BX : WIDE]
        packed = jnp.where(lane // 16 == g, pltpu.roll(tile, (8 + 16 * g) % BX, 1), packed)
    message[2 * PART : SENT, 0:BX] = packed
    for k in range(SINGLE):
        for q in range(BCOL):
            n = BCOL * k + q
            cols = slice(BX * (1 + n // 8), BX * (2 + n // 8))
            message[2 * PART + n % 8 : 2 * PART + n % 8 + 1, cols] = strip[
                2 * PART + k : 2 * PART + k + 1, BX * q : BX * q + BX
            ]


def receive(message, strip):
    strip[0 : 2 * PART, 0 : BCOL * BX] = message[0 : 2 * PART, :]
    lane = lanes((8, BX))
    inside = (lane < 8) | (lane >= BX - 8)
    packed = message[2 * PART : SENT, 0:BX]
    for g in range(STRIP // 8):
        moved = pltpu.roll(packed, (BX - 8 - 16 * g) % BX, 1)
        strip[8 * g : 8 * g + 8, BCOL * BX : WIDE] = jnp.where(inside, moved, 0.0)
    for k in range(SINGLE):
        for q in range(BCOL):
            n = BCOL * k + q
            cols = slice(BX * (1 + n // 8), BX * (2 + n // 8))
            strip[2 * PART + k : 2 * PART + k + 1, BX * q : BX * q + BX] = message[
                2 * PART + n % 8 : 2 * PART + n % 8 + 1, cols
            ]


def sums_kernel(
    thickness, blocks, tendencies, out, buffer, listed, staged, edges, weights, sems, out_sems, other_sems
):
    count = buffer.shape[0]
    nx, ny = lax.axis_size("gx"), lax.axis_size("gy")
    me = lax.axis_index("gx") * ny + lax.axis_index("gy")
    listing = pltpu.make_async_copy(blocks, listed, other_sems.at[0])
    listing.start()

    def fetch(c):
        part = pl.ds(c * CHUNK, CHUNK)
        return pltpu.make_async_copy(tendencies.at[part], buffer.at[part], sems.at[c])

    def leave(n, owner):
        return pltpu.make_async_copy(staged.at[n], out.at[owner, pl.ds(0, 2 * BY // 4)], out_sems.at[n])

    row16, lane16 = rows((BY, BX)), lanes((BY, BX))
    row4 = rows((4, BX))

    for c in range(count // CHUNK):
        fetch(c).start()
    for level in range(LEV):
        weights[level] = jnp.full((BY, BX), thickness[level], F32)
    listing.wait()

    def chunk(c, carry):
        fetch(c).wait()
        for pair in range(CHUNK // 2):
            totals = [None] * 4
            for level in range(LEV):
                weight = weights[level]
                for k in range(4):
                    n = c * CHUNK + 2 * pair + k // 2
                    term = weight * buffer[n, k % 2, level].astype(F32)
                    totals[k] = term if totals[k] is None else totals[k] + term
            for k in range(2):
                n = c * CHUNK + 2 * pair + k
                index = listed[me * count + n]
                row, col = lax.div(index, BCOL * nx), lax.rem(index, BCOL * nx)
                tile_row, tile_col, at = lax.div(row, BROW), lax.div(col, BCOL), lax.rem(col, BCOL)
                both = totals[2 * k : 2 * k + 2]
                for part in range(2):
                    staged[n, 4 * part : 4 * part + 4] = both[part].reshape(4, 4, BX)
                leave(n, tile_col * ny + tile_row).start()
                east_edge = at == BCOL - 1
                source = lane16 % 8 + jnp.where(east_edge, BX - 8, 0)
                line = []
                for value in both:
                    spread = jnp.take_along_axis(value, source, axis=1)
                    spread = jnp.where(lane16 // 8 == row16, spread, 0.0)
                    line.append(jnp.sum(spread, axis=0, keepdims=True))
                beside_col = lax.rem(tile_col + jnp.where(east_edge, 1, nx - 1), nx)
                slot = jnp.where((at == 0) | east_edge, beside_col * ny + tile_row, edges.shape[0] - 1)
                value = jnp.where(row4 % 2 == 0, line[0], line[1])
                edges[slot] = jnp.where(row4 // 2 == jnp.where(east_edge, 1, 0), value, edges[slot])
        return carry

    lax.fori_loop(0, count // CHUNK, chunk, 0)
    sides = pltpu.make_async_copy(edges.at[pl.ds(0, nx * ny)], out.at[:, 2 * BY // 4], other_sems.at[1])
    sides.start()

    def finish(n, carry):
        leave(n, 0).wait()
        return carry

    lax.fori_loop(0, count, finish, 0)
    sides.wait()


def prepare_kernel(mask, implicit, guess, fields, to_east, to_west, work):
    for q in range(BCOL):
        cols = slice(BX * q, BX * q + BX)
        m = mask[:, cols].astype(F32)
        work[q] = m * (STENCIL_SUM + implicit[:, cols]) + (1.0 - m)
        work[BCOL + q] = m * guess[:, cols]
    edge = jnp.zeros((OFF, BX), F32)
    for k in range(2):
        for p in range(BY):
            for q in range(BCOL):
                tile = work[BCOL * k + q, pl.ds(p, BROW, stride=BY), :]
                tile = jnp.concatenate([edge, tile, edge], axis=0)
                fields[k, p, :, BX * q : BX * q + BX] = tile
        part = slice(EXT * k, EXT * k + EXT)
        to_west[part, :] = pack([fields[k, p, :, 0:BX] for p in range(BY)], False)
        to_east[part, :] = pack([fields[k, p, :, BX * (BCOL - 1) :] for p in range(BY)], True)


def put_blocks(came, arrived, work, first_row, count, height, offset):
    row16, lane16 = rows((BY, BX)), lanes((BY, BX))
    spread = 8 * row16 + lane16 % 8

    def put(n, carry):
        block_row = jnp.clip(first_row + n, 0, BROW - 1)
        at_rows = pl.ds(n + offset, BY, stride=height)
        for col in range(BCOL):
            slot = came[block_row * BCOL + col]
            for part in range(2):
                value = arrived[slot, 4 * part : 4 * part + 4].reshape(BY, BX)
                work[(BCOL + 2) * part + col, at_rows, :] = value
        for side in range(2):
            slot = came[(BCOL + side) * BROW + block_row]
            for part in range(2):
                line = arrived[slot, 8, 2 * side + part : 2 * side + part + 1]
                value = jnp.take_along_axis(jnp.broadcast_to(line, (BY, BX)), spread, axis=1)
                work[(BCOL + 2) * part + BCOL + side, at_rows, :] = value
        return carry

    lax.fori_loop(0, count, put, 0, unroll=min(count, 10))


def right_side(work, fields, east, west, parts, r_wide, d_wide, x_wide, inverse, tall):
    height = sum(high - low for low, high in parts)
    for k, wide in enumerate((d_wide, x_wide)):
        sides = [
            jnp.concatenate([side[EXT * k + low : EXT * k + high, :] for low, high in parts], axis=0)
            for side in (east, west)
        ]
        for p in range(BY):
            at = 0
            for low, high in parts:
                wide[p, at : at + high - low, 0 : BCOL * BX] = fields[k, p, low:high, :]
                at += high - low
            wide[p, :, BCOL * BX : WIDE] = side_tile(*sides, p)
    previous = None
    for p in range(BY):
        d = d_wide[p]
        previous = jnp.where(d > 1.0, 1.0 / (d if p == 0 else d - previous), 0.0)
        inverse[p] = previous
        x = x_wide[p]
        tall[p] = x + CORNER_WEIGHT * beside(x)
    lane = lanes((height, BX))

    def forcing(part, p):
        at = slice(height * p, height * p + height)
        tiles = [work[(BCOL + 2) * part + q, at, :] for q in range(BCOL + 2)]
        tiles[BCOL] = jnp.where(lane < BX // 2, tiles[BCOL], tiles[BCOL + 1])
        value = jnp.concatenate(tiles[: BCOL + 1], axis=1)
        return jnp.where(d_wide[p] > 1.0, value, 0.0)

    last = forcing(1, BY - 1)
    south = pltpu.roll(last, 1, 0)
    for p in range(BY):
        f0 = forcing(0, p)
        f1 = forcing(1, p) if p + 1 < BY else last
        below = tall[p - 1] if p > 0 else pltpu.roll(tall[BY - 1], 1, 0)
        above = tall[p + 1] if p + 1 < BY else pltpu.roll(tall[0], height - 1, 0)
        x = x_wide[p]
        minus_a = beside(x) + (below + above) - d_wide[p] * x
        r_wide[p] = (f0 - pltpu.roll(f0, 1, 1)) + (f1 - south) + minus_a
        south = f1
    return last


def right_kernel(
    came, arrived, fields, east, west,
    r_wide, d_wide, x_wide, inverse, edges,
    work, tall,
):
    put_blocks(came, arrived, work, 0, BROW, EXT, OFF)
    last = right_side(work, fields, east, west, ((0, EXT),), r_wide, d_wide, x_wide, inverse, tall)
    t_top = tall[BY - 1, OFF + BROW - 1 : OFF + BROW, :]
    edges[0:1, :] = t_top - last[OFF + BROW - 1 : OFF + BROW, :]
    edges[1:2, :] = t_top
    edges[2:3, :] = tall[0, OFF : OFF + 1, :]
    edges[3:8, :] = jnp.zeros((5, WIDE), F32)


def ends_kernel(
    flags, came, arrived, fields, east, west, first, second,
    work, r_wide, d_wide, x_wide, inverse, tall, update, top, bottom, flipped,
):
    put_blocks(came, arrived, work, -OFF, 8, 16, 0)
    put_blocks(came, arrived, work, EXT - 8 - OFF, 8, 16, 8)
    parts = ((0, 8), (EXT - 8, EXT))
    last = right_side(work, fields, east, west, parts, r_wide, d_wide, x_wide, inverse, tall)
    at = 2 * PART
    south, north = OFF, 16 - OFF - 1
    for k, wide in enumerate((r_wide, d_wide)):
        for p in range(BY):
            part = slice(PART * k + DEPTH * p, PART * k + DEPTH * p + DEPTH)
            top[part, :] = wide[p, north : north + DEPTH, :]
            bottom[part, :] = wide[p, south : south + DEPTH, :]
    t_top = tall[BY - 1, north : north + 1, :]
    top[at + 4 : at + 5, :] = t_top - jnp.where(flags[1] == 1, 0.0, last[north : north + 1, :])
    top[at + 5 : at + 6, :] = x_wide[BY - 1, north : north + 1, :]
    bottom[at + 4 : at + 5, :] = tall[0, south : south + 1, :]
    bottom[at + 5 : at + 6, :] = x_wide[0, south : south + 1, :]

    def line():
        lower = []
        for p in range(BY):
            r = r_wide[p] if p == 0 else r_wide[p] + lower[-1]
            lower.append(r * inverse[p])
        upper = [lower[-1]]
        for p in range(BY - 2, -1, -1):
            upper.append(lower[p] + inverse[p] * upper[-1])
        return upper[::-1]

    behind = ((0, south + 1, bottom), (BY - 1, north - 1, top))
    row = rows((16, WIDE))
    strips = (row == south) | (row == north)
    for k in range(2):
        for p, s in enumerate(line()):
            u = s * (1.0 / GAMMA) if k == 0 else OMEGAS[1] * s + (GAMMA * OMEGAS[1] - 1.0) * update[p]
            update[p] = u
            t = u + CORNER_WEIGHT * beside(u)
            tall[p] = t if k == 0 else jnp.where(strips, 0.0, t)
        for p in range(BY):
            below = tall[p - 1] if p > 0 else pltpu.roll(tall[BY - 1], 1, 0)
            above = tall[p + 1] if p + 1 < BY else pltpu.roll(tall[0], 15, 0)
            u = update[p]
            r_wide[p] = r_wide[p] + (beside(u) + (below + above) - d_wide[p] * u)
        for p, n, strip in behind:
            strip[at + k : at + k + 1, :] = update[p, n : n + 1, :]
    smoothed = line()
    element = None
    for p in reversed(range(BY)):
        d = d_wide[p]
        element = jnp.where(d > 1.0, 1.0 / (d if element is None else d - element), 0.0)
    for (p, n, strip), diagonal in zip(behind, (element, inverse[BY - 1])):
        strip[at + 2 : at + 3, :] = smoothed[p][n : n + 1, :]
        strip[at + 3 : at + 4, :] = diagonal[n : n + 1, :]
        strip[at + SINGLE : STRIP, :] = jnp.zeros((STRIP - at - SINGLE, WIDE), F32)

    @pl.when(flags[1] == 1)
    def _():
        for k in range(2):
            for r in range(PART):
                flipped[PART * k + r : PART * k + r + 1, :] = top[PART * (k + 1) - 1 - r : PART * (k + 1) - r, :]
        flipped[at:STRIP, :] = top[at:STRIP, :]
        top[...] = turned(flipped[...])

    @pl.when(flags[0] == 1)
    def _():
        send(bottom, first)
        send(top, second)

    @pl.when(flags[0] == 0)
    def _():
        send(top, first)
        send(bottom, second)


def solve_kernel(
    flags, loc, r_wide, d_wide, x_wide, inverse_own, edges, first, second,
    solution, residual, slots,
    r_all, d_all, inverse, f_all, t_all, u_all, g_all, natural, south, north, sems,
):
    @pl.when(flags[0] == 1)
    def _():
        receive(first, south)
        receive(second, north)

    @pl.when(flags[0] == 0)
    def _():
        receive(second, south)
        receive(first, north)

    row = rows((EXT, WIDE))
    for k, (field, out) in enumerate(((r_wide, r_all), (d_wide, d_all))):
        for p in range(BY):
            part = slice(PART * k + DEPTH * p, PART * k + DEPTH * p + DEPTH)
            out[p] = field[p]
            out[p, OFF - DEPTH : OFF, :] = south[part, :]
            out[p, OFF + BROW : OFF + BROW + DEPTH, :] = north[part, :]
    previous = None
    for p in range(BY):
        d = jnp.concatenate([d_all[p, 0:8, :], d_all[p, EXT - 8 : EXT, :]], axis=0)
        previous = jnp.where(d > 1.0, 1.0 / (d if p == 0 else d - previous), 0.0)
        inverse[p, 0:8, :] = previous[0:8, :]
        inverse[p, 8 : EXT - 8, :] = inverse_own[p, 8 : EXT - 8, :]
        inverse[p, EXT - 8 : EXT, :] = previous[8:16, :]
    at = 2 * PART
    upward = jnp.where(flags[1] == 1, edges[1:2, :], edges[0:1, :])
    fix = jnp.where(row == OFF, south[at + 4 : at + 5, :], 0.0)
    r_all[0] = r_all[0] + jnp.where(row == OFF + BROW, upward, fix)
    fix = jnp.where(row == OFF + BROW - 1, north[at + 4 : at + 5, :], 0.0)
    r_all[BY - 1] = r_all[BY - 1] + jnp.where(row == OFF - 1, edges[2:3, :], fix)

    def gathered(p, k):
        below = t_all[p - 1] if p > 0 else pltpu.roll(t_all[BY - 1], 1, 0)
        above = t_all[p + 1] if p + 1 < BY else pltpu.roll(t_all[0], EXT - 1, 0)
        if k < ITERS:
            at_k = slice(at + k - 1, at + k)
            if p == 0:
                u = south[at_k, :]
                below = jnp.where(row == OFF - 1, u + CORNER_WEIGHT * beside(u), below)
            if p == BY - 1:
                u = north[at_k, :]
                above = jnp.where(row == OFF + BROW, u + CORNER_WEIGHT * beside(u), above)
        return r_all[p] + (below + above)

    for k, omega in enumerate(OMEGAS):
        f = None
        for p in range(BY):
            if k > 0:
                r = gathered(p, k)
                r_all[p] = r
            else:
                r = r_all[p]
            f = (r if f is None else r + f) * inverse[p]
            f_all[p] = f
        s = None
        for p in reversed(range(BY)):
            s = f_all[p] if s is None else f_all[p] + inverse[p] * s
            if k == 0:
                u = s * (1.0 / GAMMA)
            else:
                u = omega * s + (GAMMA * omega - 1.0) * u_all[k - 1, p]
            u_all[k, p] = u
            h = beside(u)
            t_all[p] = u + CORNER_WEIGHT * h
            r_all[p] = r_all[p] + (h - d_all[p] * u)
        if k == 1:
            for strip, p, n in ((south, 0, OFF - 1), (north, BY - 1, OFF + BROW)):
                s = strip[at + 2 : at + 3, :] + strip[at + 3 : at + 4, :] * t_all[p, n : n + 1, :]
                u = OMEGAS[2] * s + (GAMMA * OMEGAS[2] - 1.0) * strip[at + 1 : at + 2, :]
                strip[at + 2 : at + 3, :] = u
    for p in range(BY):
        r = jnp.where(d_all[p] > 1.0, gathered(p, ITERS), 0.0)
        start = x_wide[p]
        if p == 0:
            start = jnp.where(row == OFF + BROW, north[at + 5 : at + 6, :], start)
        x = start + ((u_all[0, p] + u_all[1, p]) + (u_all[2, p] + u_all[3, p]))
        f_all[p] = x
        for q in range(BCOL):
            cols = slice(BX * q, BX * q + BX)
            natural[q, pl.ds(p, BROW, stride=BY), :] = x[OFF : OFF + BROW, cols]
            natural[BCOL + q, pl.ds(p, BROW, stride=BY), :] = r[OFF : OFF + BROW, cols]
    copies = []
    for k, out in enumerate((solution, residual)):
        for q in range(BCOL):
            n = BCOL * k + q
            copies.append(pltpu.make_async_copy(natural.at[n], out.at[:, pl.ds(BX * q, BX)], sems.at[n]))
    for copy in copies:
        copy.start()
    for p in range(BY):
        x = f_all[p]
        ocean = d_all[p] > 1.0
        above = f_all[p + 1] if p + 1 < BY else pltpu.roll(f_all[0], EXT - 1, 0)
        zonal = jnp.where(ocean, pltpu.roll(x, WIDE - 1, 1) - x, 0.0)
        meridional = jnp.where(ocean, above - x, 0.0)
        for q in range(BCOL):
            cols = slice(BX * q, BX * q + BX)
            g_all[q, EXT * p : EXT * p + EXT, :] = zonal[:, cols]
            g_all[BCOL + q, EXT * p : EXT * p + EXT, :] = meridional[:, cols]

    def take(slot, carry):
        index = loc[slot]
        row, col = (index >> 2) + OFF, index & 3
        slots[slot, 0] = g_all[col, pl.ds(row, BY, stride=EXT), :]
        slots[slot, 1] = g_all[BCOL + col, pl.ds(row, BY, stride=EXT), :]
        return carry

    lax.fori_loop(0, slots.shape[0], take, 0, unroll=16)
    for copy in copies:
        copy.wait()


def pick_kernel(dst, slots, out, picked, sems):
    part = picked.shape[0] // sems.shape[0]
    copies = []
    for c in range(sems.shape[0]):
        for n in range(part * c, part * c + part):
            picked[n] = slots[dst[n]]
        at = pl.ds(part * c, part)
        copies.append(pltpu.make_async_copy(picked.at[at], out.at[at], sems.at[c]))
        copies[-1].start()
    for copy in copies:
        copy.wait()


def body(tendencies, thickness, ocean_blocks, land_mask, implicit_term, first_guess):
    nx = lax.axis_size("gx")
    ny = lax.axis_size("gy")
    gx = lax.axis_index("gx")
    gy = lax.axis_index("gy")
    devices = nx * ny
    listed = tendencies.shape[0]
    me = gx * ny + gy
    block_cols = BCOL * nx
    block_row = ocean_blocks // block_cols
    block_col = ocean_blocks % block_cols
    owner = block_col // BCOL * ny + block_row // BROW
    local = block_row % BROW * BCOL + block_col % BCOL
    dst = lax.dynamic_slice_in_dim(owner, me * listed, listed)
    loc = jnp.min(jnp.where(owner == me, local, BROW * BCOL).reshape(devices, listed), axis=1)
    device = jnp.arange(devices, dtype=jnp.int32)
    came = [(loc[None, :] == jnp.arange(BROW * BCOL, dtype=jnp.int32)[:, None])]
    for step, at in ((1, 0), (nx - 1, BCOL - 1)):
        here = (owner == (gx + step) % nx * ny + gy) & (local % BCOL == at)
        side = jnp.min(jnp.where(here, local // BCOL, BROW).reshape(devices, listed), axis=1)
        came.append(side[None, :] == jnp.arange(BROW, dtype=jnp.int32)[:, None])
    came = jnp.max(jnp.where(jnp.concatenate(came), device[None, :], 0), axis=1)
    flags = jnp.stack([gy % 2, (gy == ny - 1).astype(jnp.int32)]).astype(jnp.int32)

    east = [(i, (i + 1) % nx) for i in range(nx)]
    west = [(j, i) for i, j in east]
    swap_a, swap_b = [], []
    for i in range(nx):
        for j in range(ny):
            swap_a.append((i * ny + j, i * ny + (j ^ 1)))
            if j == ny - 1:
                swap_b.append((i * ny + j, (nx - 1 - i) * ny + j))
            elif j > 0:
                swap_b.append((i * ny + j, i * ny + (j + 1 if j % 2 else j - 1)))

    def exchange_x(to_east, to_west):
        return lax.ppermute(to_west, "gx", west), lax.ppermute(to_east, "gx", east)

    hbm = pl.BlockSpec(memory_space=pltpu.HBM)
    back = (devices, 2, BY, BX)
    sums = pl.pallas_call(
        sums_kernel,
        out_shape=jax.ShapeDtypeStruct((devices, 2 * BY // 4 + 1, 4, BX), F32),
        in_specs=[pl.BlockSpec(memory_space=pltpu.SMEM), hbm, hbm],
        out_specs=hbm,
        scratch_shapes=[
            pltpu.VMEM(tendencies.shape, tendencies.dtype),
            pltpu.SMEM(ocean_blocks.shape, jnp.int32),
            pltpu.VMEM((listed, 2 * BY // 4, 4, BX), F32),
            pltpu.VMEM((devices + 1, 4, BX), F32),
            pltpu.VMEM((LEV, BY, BX), F32),
            pltpu.SemaphoreType.DMA((listed // CHUNK,)),
            pltpu.SemaphoreType.DMA((listed,)),
            pltpu.SemaphoreType.DMA((2,)),
        ],
        compiler_params=pltpu.CompilerParams(vmem_limit_bytes=58 * MIB),
    )(thickness, ocean_blocks, tendencies)
    arrived = lax.all_to_all(sums, ("gx", "gy"), split_axis=0, concat_axis=0, tiled=True)

    own = (BY, EXT, BCOL * BX)
    tile = (BROW * BY, BCOL * BX)
    full = (BY, EXT, WIDE)
    strip = (STRIP, WIDE)
    sent = (SENT, BCOL * BX)
    sums, land_mask, implicit_term, first_guess = lax.optimization_barrier(
        (sums, land_mask, implicit_term, first_guess)
    )
    fields, to_east, to_west = call(
        prepare_kernel,
        [(2, *own), (2 * EXT, BX), (2 * EXT, BX)],
        [land_mask, implicit_term, first_guess],
        [(2 * BCOL + 1, BROW * BY, BX)],
        58,
    )
    from_sides = exchange_x(to_east, to_west)

    small = (BY, 16, WIDE)
    first, second = call(
        ends_kernel,
        [sent, sent],
        [flags, came, arrived, fields, *from_sides],
        [(2 * (BCOL + 2), BY * 16, BX), small, small, small, small, small, small, strip, strip, strip],
        12,
    )
    came, first, second = lax.optimization_barrier((came, first, second))
    first = lax.ppermute(first, ("gx", "gy"), swap_a)
    second = lax.ppermute(second, ("gx", "gy"), swap_b)
    r_wide, d_wide, x_wide, inverse, edges = call(
        right_kernel,
        [full, full, full, full, (8, WIDE)],
        [came, arrived, fields, *from_sides],
        [(2 * (BCOL + 2), BY * EXT, BX), full],
        12,
    )
    vmem = pl.BlockSpec(memory_space=pltpu.VMEM)
    smem = pl.BlockSpec(memory_space=pltpu.SMEM)
    solution, residual, slots = pl.pallas_call(
        solve_kernel,
        out_shape=[jax.ShapeDtypeStruct(a, F32) for a in (tile, tile, back)],
        in_specs=[smem, smem] + [vmem] * 7,
        out_specs=[hbm, hbm, vmem],
        scratch_shapes=[pltpu.VMEM(full, F32)] * 5
        + [
            pltpu.VMEM((ITERS, *full), F32),
            pltpu.VMEM((2 * BCOL, BY * EXT, BX), F32),
            pltpu.VMEM((2 * BCOL + 1, BROW * BY, BX), F32),
            pltpu.VMEM(strip, F32),
            pltpu.VMEM(strip, F32),
            pltpu.SemaphoreType.DMA((2 * BCOL,)),
        ],
        compiler_params=pltpu.CompilerParams(vmem_limit_bytes=18 * MIB),
    )(flags, loc, r_wide, d_wide, x_wide, inverse, edges, first, second)
    returned = lax.all_to_all(slots, ("gx", "gy"), split_axis=0, concat_axis=0, tiled=True)
    gradient_blocks = pl.pallas_call(
        pick_kernel,
        out_shape=jax.ShapeDtypeStruct((listed, 2, BY, BX), F32),
        in_specs=[pl.BlockSpec(memory_space=pltpu.SMEM), pl.BlockSpec(memory_space=pltpu.VMEM)],
        out_specs=pl.BlockSpec(memory_space=pl.ANY),
        scratch_shapes=[pltpu.VMEM((listed, 2, BY, BX), F32), pltpu.SemaphoreType.DMA((4,))],
        compiler_params=pltpu.CompilerParams(vmem_limit_bytes=4 * MIB),
    )(dst, returned)
    return solution, residual, gradient_blocks


def solution(mesh):
    placed = (
        P(("gx", "gy"), None, None, None, None),
        P(),
        P(),
        P("gy", "gx"),
        P("gy", "gx"),
        P("gy", "gx"),
    )
    return jax.shard_map(
        body,
        mesh=mesh,
        in_specs=placed,
        out_specs=(P("gy", "gx"), P("gy", "gx"), P(("gx", "gy"), None, None, None)),
        check_vma=False,
    )
```
